256 devices in a mesh: vocab: 16 (over z_lo, y, core), units: 16 (over x, z_hi).
Axes of the slice: x: 4, y: 4, z: 8 (z_hi: 4, z_lo: 2; z = z_hi * 2 + z_lo), core: 2. Of those that a mesh axis runs over, the one named last changes fastest.
Arguments:
- x_rows: bfloat16 [16, 16, 32, 1024], P('vocab', 'units'), may hold values from -16 to 16
- gain_in: float32 [1024], replicated, may hold values from 0.1 to 1.9
- w_in: bfloat16 [1024, 32768], P(None, 'units'), may hold values from -0.1875 to 0.1875
- w_out: bfloat16 [32768, 1024], P('units'), may hold values from -0.03125 to 0.03125
- gain_out: float32 [1024], replicated, may hold values from 0.1 to 1.9
- embed: bfloat16 [32256, 1024], P('vocab'), may hold values from -600 to 600
- targets: int32 [16, 16, 32], P(None, 'units'), may hold values from 0 to 32127
- row_mask: int32 [16, 16, 32], P(None, 'units'), may hold values 0 or 1
Outputs:
- grad_x: float32 [16, 16, 32, 1024], P('vocab', 'units')
The draws below stay inside these ranges and needn't reach their ends.
Inputs may be any that keep to these rules, and one draw needn't show every extreme that they name: `targets`: ids of live vocabulary entries.
All inputs are finite; a program needn't handle non-finite values. No bound on the sum of `row_mask` on one device may be relied on, other than what follows from the above.
Results may differ from the reference program's by a relative error of at most 0.02.
The reference program's roundings to bfloat16 on the way (of `normed`, `active`, `final_rows`, `grad_logits`, `grad_half` and `grad_active`) count: a program that leaves them out, or rounds other values in their place, can miss the bound.
Values may be sent and summed in bfloat16 or wider, within the bound.
A program may use at most 64 MiB of HBM per device.

```python
import math
import jax
import jax.numpy as jnp
import numpy as np
from jax import lax

D = 1024
FF = 32768
VOCAB = 32128
VOCAB_PAD = 32256
BLOCK = 32
NVOC = 16
NUNIT = 16


def shared_directions(key):
    directions = jax.random.normal(jax.random.fold_in(key, 101), (8, D), jnp.float32)
    return directions


def draw_x_rows(key, part):
    directions = shared_directions(key)
    key = jax.random.fold_in(key, 11)
    key_a, key_b, key_c = jax.random.split(key, 3)
    shape = (NVOC, NUNIT, BLOCK, D)
    noise = jax.random.normal(key_a, shape, jnp.float32)
    pick = jax.random.randint(key_b, (NVOC, NUNIT, BLOCK), 0, 8)
    strength = jax.random.uniform(key_c, (NVOC, NUNIT, BLOCK, 1), jnp.float32, 0.55, 0.65)
    rows = 0.8 * noise + strength * directions[pick]
    return jnp.clip(rows, -16.0, 16.0).astype(jnp.bfloat16)


def draw_embed(key, part):
    directions = shared_directions(key)
    key = jax.random.fold_in(key, 7)
    key_a = jax.random.fold_in(key, 0)
    key_b = jax.random.fold_in(key, 1)
    key_c = jax.random.fold_in(key, 2)
    key_e = jax.random.fold_in(key, 4)
    index = jnp.arange(VOCAB_PAD, dtype=jnp.float32)[:, None]
    jitter = jnp.exp(jax.random.uniform(key_b, (VOCAB_PAD, 1), jnp.float32, -0.2, 0.2))
    sigma = (0.55 + 0.9 * index / VOCAB_PAD) * jitter
    noise = jax.random.normal(key_a, (VOCAB_PAD, D), jnp.float32)
    offset = 3.0 * jax.random.normal(key_c, (1, D), jnp.float32)
    table = sigma * noise + offset
    picks = jax.random.permutation(key_e, VOCAB)[:14]
    height = (math.log(VOCAB) + 1.8) * 1.22 / 0.6
    peaks = height * directions / math.sqrt(D) + offset
    table = table.at[picks[:8]].set(peaks)
    return jnp.clip(table, -600.0, 600.0).astype(jnp.bfloat16)


def with_ends(values, rng, smallest, high):
    longest = values.shape.index(max(values.shape))
    spots = []
    for shift in (0, 1):
        where = [jax.random.randint(jax.random.fold_in(rng, axis), (), 0, length) for axis, length in enumerate(values.shape)]
        where[longest] = (where[longest] + shift) % values.shape[longest]
        spots.append(tuple(where))
    return values.at[spots[0]].set(smallest).at[spots[1]].set(high)


def block_scale(own_key, extent, cuts, smallest, largest):
    factor_of, own = 1.0, jax.random.fold_in(own_key, 6)
    for dim, blocks in cuts:
        heights = jnp.exp(jax.random.uniform(jax.random.fold_in(own, dim), (blocks,), jnp.float32, smallest / len(cuts), largest / len(cuts)))
        factor_of = factor_of * jnp.repeat(heights, extent[dim] // blocks).reshape([-1 if axis == dim else 1 for axis in range(len(extent))])
    return factor_of


def rank_bounds(number_of, lean):
    weights = [(1 << 20) // math.isqrt(standing ** lean) + 1 for standing in range(1, number_of + 1)]
    scale = 1 + sum(weights) // (1 << 30)
    return np.cumsum(np.array([max(1, weight // scale) for weight in weights]))


def skewed_ids(stream_key, extent, number_of, skew):
    table = rank_bounds(number_of, skew)
    ticket = jax.random.randint(jax.random.fold_in(stream_key, 1), extent, 0, int(table[number_of - 1]))
    standing = jnp.searchsorted(jnp.asarray(table, jnp.int32), ticket, side="right")
    return jax.random.permutation(jax.random.fold_in(stream_key, 2), number_of)[standing].astype(jnp.int32)


def bell_draw(own_key, dims, spread, reach, cuts=(), held_as=jnp.bfloat16):
    loudness = block_scale(own_key, dims, cuts, -0.22, 0.18) if cuts else 1.0
    drawn = jax.random.normal(own_key, dims, jnp.float32) * spread * loudness
    return jnp.minimum(jnp.maximum(drawn, -reach), reach).astype(held_as)


def setup_inputs(seed: int = 0) -> dict:
    streams_of = jax.random.split(jax.random.key(seed), 9)
    return {
        "x_rows": draw_x_rows(jax.random.fold_in(streams_of[8], 71), 0),
        "gain_in": jnp.clip(1.0 + 0.18 * jax.random.normal(streams_of[1], (D,), jnp.float32), 0.1, 1.9),
        "w_in": bell_draw(streams_of[2], (D, FF), D ** -0.5, 0.1875, ((1, 16),)),
        "w_out": bell_draw(streams_of[3], (FF, D), FF ** -0.5, 0.03125, ((0, 16),)),
        "gain_out": jnp.clip(1.0 + 0.18 * jax.random.normal(streams_of[4], (D,), jnp.float32), 0.1, 1.9),
        "embed": draw_embed(jax.random.fold_in(streams_of[8], 71), 0),
        "targets": with_ends(skewed_ids(streams_of[6], (NVOC, NUNIT, BLOCK), VOCAB, 2), jax.random.fold_in(streams_of[6], 3), 0, VOCAB - 1).astype(jnp.int32),
        "row_mask": with_ends((jax.random.randint(streams_of[7], (NVOC, NUNIT, BLOCK), 0, 4) < 3).astype(jnp.int32), jax.random.fold_in(streams_of[7], 1), 0, 1),
    }


EPSILON = 1e-06

def norm_scale(values):
    return lax.rsqrt(lax.optimization_barrier(jnp.mean(values * values, axis=-1, keepdims=True)) + EPSILON)

def norm_back(grad_in, values, scale_rows, gain_vec):
    scaled = grad_in * gain_vec
    inner_sum = lax.optimization_barrier(jnp.mean(scaled * values, axis=-1, keepdims=True))
    return scaled * scale_rows - values * (scale_rows * scale_rows * scale_rows) * inner_sum

def reference(x_rows, gain_in, w_in, w_out, gain_out, embed, targets, row_mask):
    factor = 1.0 / math.sqrt(D)
    columns = jnp.arange(VOCAB_PAD, dtype=jnp.int32)[None, :]
    live_cols = columns < VOCAB

    def group_grad(packed):
        block_x, block_labels, block_mask = packed
        inputs = block_x.reshape(-1, D).astype(jnp.float32)
        scale_in = norm_scale(inputs)
        normed = (inputs * scale_in * gain_in).astype(jnp.bfloat16)
        before = jnp.dot(normed, w_in, preferred_element_type=jnp.float32)
        active = jnp.maximum(before, 0.0).astype(jnp.bfloat16)
        summed = inputs + jnp.dot(active, w_out, preferred_element_type=jnp.float32)
        scale_out = norm_scale(summed)
        final_rows = (summed * scale_out * gain_out).astype(jnp.bfloat16)
        logits = jnp.dot(final_rows, embed.T, preferred_element_type=jnp.float32) * factor
        logits = jnp.where(live_cols, logits, -1e+30)
        top_value = lax.optimization_barrier(jnp.max(logits, axis=1, keepdims=True))
        shifted = jnp.exp(logits - top_value)
        probability = shifted / lax.optimization_barrier(jnp.sum(shifted, axis=1, keepdims=True))
        labels = block_labels.reshape(-1)
        weights = block_mask.reshape(-1).astype(jnp.float32)
        onehot = (columns == labels[:, None]).astype(jnp.float32)
        grad_logits = (weights[:, None] * (probability - onehot)).astype(jnp.bfloat16)
        grad_final = jnp.dot(grad_logits, embed, preferred_element_type=jnp.float32) * factor
        grad_sum = norm_back(grad_final, summed, scale_out, gain_out)
        grad_half = grad_sum.astype(jnp.bfloat16)
        product = jnp.dot(grad_half, w_out.T, preferred_element_type=jnp.float32)
        grad_active = jnp.where(before > 0, product, 0.0).astype(jnp.bfloat16)
        grad_normed = jnp.dot(grad_active, w_in.T, preferred_element_type=jnp.float32)
        result = grad_sum + norm_back(grad_normed, inputs, scale_in, gain_in)
        return result.reshape(block_x.shape)
    return lax.map(group_grad, (x_rows, targets, row_mask))
```

```python
import functools
import math

import jax
import jax.numpy as jnp
from jax import lax
from jax.experimental import pallas as pl
from jax.experimental.pallas import tpu as pltpu
from jax.sharding import PartitionSpec as P

D = 1024
VOCAB = 32128
EPSILON = 1e-06
CHUNKS = 2
F32, BF16 = jnp.float32, jnp.bfloat16
MESH = pl.DeviceIdType.MESH
STEPS = (2, 1, 3)
CHIP_STEPS = ((1, 2), (0, 2), (1, 1), (1, 3), (0, 1), (0, 3), (1, 0))
PEER_STEPS = tuple(s + (c,) for s in CHIP_STEPS for c in (0, 1)) + ((0, 0, 1),)
NT = (((1,), (1,)), ((), ()))


def norm_scale(values):
    return lax.rsqrt(jnp.mean(values * values, axis=-1, keepdims=True) + EPSILON)


def norm_back(grad_in, values, scale_rows, gain_vec):
    scaled = grad_in * gain_vec
    inner_sum = jnp.mean(scaled * values, axis=-1, keepdims=True)
    return scaled * scale_rows - values * (scale_rows * scale_rows * scale_rows) * inner_sum


def eye(rows, columns, shift=0):
    row = lax.broadcasted_iota(jnp.int32, (rows, columns), 0)
    return row + shift == lax.broadcasted_iota(jnp.int32, (rows, columns), 1)


def as_row(column):
    return jnp.sum(jnp.where(eye(128, 128), column, 0.0), axis=0, keepdims=True)


def as_column(row, mask):
    return jnp.sum(jnp.where(mask, row, 0.0), axis=1, keepdims=True)


def kernel(
    x_ref, gain_in_ref, w_in_hbm, w_out_hbm, gain_out_ref, embed_hbm, targets_ref, mask_ref,
    out_ref,
    w_in, w_out, embed, near, active, logits, grads, label, weight,
    fwd_all, fwd_part, fwd_own, fwd_x, fwd_mid, fwd_z,
    head_all, stats, stats_in, head_part, head_core, head_mid, head_in,
    bwd_all, bwd_part, bwd_own, bwd_x, bwd_mid, bwd_z,
    summed_ref, grad_sum_ref, local_sem, send_sem, recv_sem,
):
    vocab = lax.axis_index("vocab")
    unit = lax.axis_index("units")
    x_at, z_at = unit // 4, unit % 4
    core, y_at, zlo_at = vocab % 2, (vocab // 2) % 4, vocab // 8
    local_vocab = embed_hbm.shape[0]
    padded_vocab = embed.shape[0]
    block = x_ref.shape[0]
    part = block // CHUNKS
    rows = 16 * part
    hidden = w_in.shape[1]
    factor = 1.0 / math.sqrt(D)
    chunks = range(CHUNKS)

    def unit_peer(dx, dz):
        return vocab, ((x_at + dx) % 4) * 4 + (z_at + dz) % 4

    def vocab_peer(dzlo, dy, dcore):
        return ((zlo_at + dzlo) % 2) * 8 + ((y_at + dy) % 4) * 2 + (core + dcore) % 2, unit

    def chip_slot(dzlo, dy):
        return ((zlo_at + dzlo) % 2) * 4 + (y_at + dy) % 4

    def take(start, size):
        return pl.ds(pl.multiple_of(start, size), size)

    used = [0]
    started = []

    def send(src, dst, peer):
        k = used[0]
        used[0] += 1
        copy = pltpu.make_async_remote_copy(
            src_ref=src, dst_ref=dst, send_sem=send_sem.at[k], recv_sem=recv_sem.at[k],
            device_id=peer, device_id_type=MESH,
        )
        copy.start()
        started.append(copy)
        return copy

    loads = [
        pltpu.make_async_copy(w_in_hbm, w_in, local_sem.at[0]),
        pltpu.make_async_copy(w_out_hbm, w_out, local_sem.at[1]),
        pltpu.make_async_copy(embed_hbm, embed.at[pl.ds(0, local_vocab)], local_sem.at[2]),
    ]
    for load in loads:
        load.start()

    barrier = pltpu.get_barrier_semaphore()
    greet = [unit_peer(d, 0) for d in STEPS] + [unit_peer(0, d) for d in STEPS]
    greet += [vocab_peer(*s) for s in PEER_STEPS]
    for peer in greet:
        pl.semaphore_signal(barrier, inc=1, device_id=peer, device_id_type=MESH)

    inputs = x_ref[...].astype(F32)
    scale_in = norm_scale(inputs)
    normed = (inputs * scale_in * gain_in_ref[...]).astype(BF16)
    for c in chunks:
        fwd_all[c, 0:part, :] = normed[c * part : (c + 1) * part]
    embed[local_vocab:, :] = jnp.zeros((padded_vocab - local_vocab, D), BF16)
    pl.semaphore_wait(barrier, len(greet))

    def unit_gather_start(buf):
        along_z = [
            send(buf.at[pl.ds(0, part)], buf.at[pl.ds((4 - d) * part, part)], unit_peer(0, d))
            for d in STEPS
        ]
        along_x = [
            send(buf.at[pl.ds(0, part)], buf.at[pl.ds((4 - d) * 4 * part, part)], unit_peer(d, 0))
            for d in STEPS
        ]
        return along_z, along_x

    def unit_gather_pass(buf, along_z, along_x):
        for copy in along_z:
            copy.wait_recv()
        return along_x + [
            send(
                buf.at[pl.ds(part, 3 * part)],
                buf.at[pl.ds(((4 - d) * 4 + 1) * part, 3 * part)],
                unit_peer(d, 0),
            )
            for d in STEPS
        ]

    def unit_sum_start(partial, landing):
        return [
            send(partial.at[pl.ds(d * 4 * part, 4 * part)], landing.at[d - 1], unit_peer(d, 0))
            for d in STEPS
        ]

    def unit_sum_pass(copies, own, landing, mid, landing_z):
        for copy in copies:
            copy.wait_recv()
        total = own[...]
        for d in (1, 2, 3):
            total = total + landing[d - 1].astype(F32)
        own[...] = total
        mid[...] = total.astype(BF16)
        return [
            send(mid.at[pl.ds(d * part, part)], landing_z.at[d - 1], unit_peer(0, d))
            for d in STEPS
        ]

    def unit_sum_end(copies, own, landing_z):
        for copy in copies:
            copy.wait_recv()
        total = own[0:part, :]
        for d in (1, 2, 3):
            total = total + landing_z[d - 1].astype(F32)
        return total

    fwd = [unit_gather_start(fwd_all.at[c]) for c in chunks]

    for c in chunks:
        pick = eye(part, block, c * part)
        for slot in range(16):
            owner = ((slot // 4) % 2) * 8 + (slot % 4) * 2 + slot // 8
            label[c, slot * part : (slot + 1) * part, :] = as_column(
                targets_ref[owner].astype(F32), pick
            )
            weight[c, slot * part : (slot + 1) * part, :] = as_column(
                mask_ref[owner].astype(F32), pick
            )

    fwd = [unit_gather_pass(fwd_all.at[c], *fwd[c]) for c in chunks]

    fwd_sum = []
    for c in chunks:
        if c == 0:
            loads[0].wait()
        for copy in fwd[c]:
            copy.wait_recv()

        @pl.loop(0, hidden // 512)
        def _(j):
            at = take(j * 512, 512)
            before = jnp.dot(fwd_all[c], w_in[:, at], preferred_element_type=F32)
            active[c, :, at] = jnp.maximum(before, 0.0).astype(BF16)

        if c == 0:
            loads[1].wait()

        @pl.loop(0, D // 512)
        def _(j):
            at = take(j * 512, 512)
            product = jnp.dot(active[c], w_out[:, at], preferred_element_type=F32)
            fwd_own[c, :, at] = product[0 : 4 * part]
            fwd_part[c, :, at] = product.astype(BF16)

        fwd_sum.append(unit_sum_start(fwd_part.at[c], fwd_x.at[c]))

    fwd_sum = [
        unit_sum_pass(fwd_sum[c], fwd_own.at[c], fwd_x.at[c], fwd_mid.at[c], fwd_z.at[c])
        for c in chunks
    ]

    my_slot = core * 8 + chip_slot(0, 0)
    head = []
    for c in chunks:
        summed = inputs[c * part : (c + 1) * part] + unit_sum_end(
            fwd_sum[c], fwd_own.at[c], fwd_z.at[c]
        )
        summed_ref[c] = summed
        final = (summed * norm_scale(summed) * gain_out_ref[...]).astype(BF16)
        mine = head_all.at[c, take(my_slot * part, part)]
        mine[...] = final
        head.append([send(mine, mine, vocab_peer(*s, 0)) for s in CHIP_STEPS])
        head[c].append(send(mine, mine, vocab_peer(0, 0, 1)))

    loads[2].wait()
    lane = lax.broadcasted_iota(jnp.int32, (1, 512), 1)
    exchange = []
    top = []
    for c in chunks:
        across = [head[c][-1]]
        for copy, (dzlo, dy) in reversed(list(zip(head[c][:-1], CHIP_STEPS))):
            copy.wait_recv()
            slot = head_all.at[c, take((core * 8 + chip_slot(-dzlo, -dy)) * part, part)]
            across.append(send(slot, slot, vocab_peer(0, 0, 1)))
        for copy in across:
            copy.wait_recv()

        def logits_tile(j, best):
            at = take(j * 512, 512)
            tile = lax.dot_general(head_all[c], embed[at, :], NT, preferred_element_type=F32)
            here = lane + j * 512
            live = jnp.logical_and(here < local_vocab, here + vocab * local_vocab < VOCAB)
            tile = jnp.where(live, tile * factor, -1e30)
            logits[c, :, at] = tile
            for k in range(4):
                best = jnp.maximum(best, tile[:, k * 128 : (k + 1) * 128])
            return best

        best = lax.fori_loop(
            0, padded_vocab // 512, logits_tile, jnp.full((rows, 128), -1e30, F32)
        )
        local_top = jnp.max(best, axis=1, keepdims=True)

        def exp_tile(j, acc):
            at = take(j * 512, 512)
            tile = jnp.exp(logits[c, :, at] - local_top)
            logits[c, :, at] = tile
            for k in range(4):
                acc = acc + tile[:, k * 128 : (k + 1) * 128]
            return acc

        acc = lax.fori_loop(0, padded_vocab // 512, exp_tile, jnp.zeros((rows, 128), F32))
        local_sum = jnp.sum(acc, axis=1, keepdims=True)
        halves = rows // 128
        stats[c] = jnp.zeros((8, 128), F32)
        for h in range(halves):
            stats[c, h : h + 1, :] = as_row(local_top[h * 128 : (h + 1) * 128])
            stats[c, 4 + h : 5 + h, :] = as_row(local_sum[h * 128 : (h + 1) * 128])
        exchange.append(
            [send(stats.at[c], stats_in.at[c, k], vocab_peer(*s)) for k, s in enumerate(PEER_STEPS)]
        )

    head_sum = []
    for c in chunks:
        for copy in exchange[c]:
            copy.wait_recv()
        own_top, own_sum = stats[c, 0:4, :], stats[c, 4:8, :]
        row_top = own_top
        for k in range(len(PEER_STEPS)):
            row_top = jnp.maximum(row_top, stats_in[c, k, 0:4, :])
        row_sum = own_sum * jnp.exp(own_top - row_top)
        for k in range(len(PEER_STEPS)):
            row_sum = row_sum + stats_in[c, k, 4:8, :] * jnp.exp(stats_in[c, k, 0:4, :] - row_top)
        ratio_rows = jnp.exp(own_top - row_top) / row_sum
        ratio = jnp.concatenate(
            [as_column(ratio_rows[h : h + 1], eye(128, 128)) for h in range(rows // 128)], axis=0
        )
        wanted = label[c].astype(jnp.int32) - vocab * local_vocab

        @pl.loop(0, padded_vocab // 512)
        def _(j):
            at = take(j * 512, 512)
            onehot = (lane + j * 512 == wanted).astype(F32)
            grads[c, :, at] = (weight[c] * (logits[c, :, at] * ratio - onehot)).astype(BF16)

        @pl.loop(0, D // 512)
        def _(j):
            at = take(j * 512, 512)
            product = jnp.dot(grads[c], embed[:, at], preferred_element_type=F32) * factor
            head_part[c, :, at] = product.astype(BF16)

        half = rows // 2
        head_sum.append(
            send(
                head_part.at[c, take((1 - core) * half, half)], head_core.at[c],
                vocab_peer(0, 0, 1),
            )
        )

    for c in chunks:
        head_sum[c].wait_recv()
        half = rows // 2
        total = head_part[c, take(core * half, half), :].astype(F32) + head_core[c].astype(F32)
        head_mid[c] = total.astype(BF16)
        head_sum[c] = [
            send(
                head_mid.at[c, take(chip_slot(*s) * part, part)], head_in.at[c, k],
                vocab_peer(*s, 0),
            )
            for k, s in enumerate(CHIP_STEPS)
        ]

    bwd = []
    for c in chunks:
        for copy in head_sum[c]:
            copy.wait_recv()
        grad_final = head_mid[c, take(chip_slot(0, 0) * part, part), :].astype(F32)
        for k in range(len(CHIP_STEPS)):
            grad_final = grad_final + head_in[c, k].astype(F32)
        summed = summed_ref[c]
        grad_sum = norm_back(grad_final, summed, norm_scale(summed), gain_out_ref[...])
        grad_sum_ref[c] = grad_sum
        bwd_all[c, 0:part, :] = grad_sum.astype(BF16)
        bwd.append(unit_gather_start(bwd_all.at[c]))
    bwd = [unit_gather_pass(bwd_all.at[c], *bwd[c]) for c in chunks]

    bwd_sum = []
    for c in chunks:
        for copy in bwd[c]:
            copy.wait_recv()

        @pl.loop(0, hidden // 512)
        def _(j):
            at = take(j * 512, 512)
            product = lax.dot_general(bwd_all[c], w_out[at, :], NT, preferred_element_type=F32)
            held = active[c, :, at]
            near[c, :, at] = jnp.where(held.astype(F32) > 0.0, product, 0.0).astype(BF16)

        @pl.loop(0, D // 512)
        def _(j):
            at = take(j * 512, 512)
            product = lax.dot_general(near[c], w_in[at, :], NT, preferred_element_type=F32)
            bwd_own[c, :, at] = product[0 : 4 * part]
            bwd_part[c, :, at] = product.astype(BF16)

        bwd_sum.append(unit_sum_start(bwd_part.at[c], bwd_x.at[c]))

    bwd_sum = [
        unit_sum_pass(bwd_sum[c], bwd_own.at[c], bwd_x.at[c], bwd_mid.at[c], bwd_z.at[c])
        for c in chunks
    ]
    for c in chunks:
        grad_normed = unit_sum_end(bwd_sum[c], bwd_own.at[c], bwd_z.at[c])
        here = slice(c * part, (c + 1) * part)
        out_ref[here, :] = grad_sum_ref[c] + norm_back(
            grad_normed, inputs[here], scale_in[here], gain_in_ref[...]
        )
    for copy in started:
        copy.wait_send()


def local(x_rows, gain_in, w_in, w_out, gain_out, embed, targets, row_mask):
    block = x_rows.shape[2]
    part = block // CHUNKS
    rows = 16 * part
    hidden = w_in.shape[1]
    padded_vocab = (embed.shape[0] + 511) // 512 * 512
    c = CHUNKS
    unit_sum = [
        pltpu.VMEM((c, rows, D), BF16),
        pltpu.VMEM((c, rows, D), BF16),
        pltpu.VMEM((c, 4 * part, D), F32),
        pltpu.VMEM((c, 3, 4 * part, D), BF16),
        pltpu.VMEM((c, 4 * part, D), BF16),
        pltpu.VMEM((c, 3, part, D), BF16),
    ]
    scratch = [
        pltpu.VMEM(w_in.shape, BF16),
        pltpu.VMEM(w_out.shape, BF16),
        pltpu.VMEM((padded_vocab, D), BF16),
        pltpu.VMEM((c, rows, hidden), BF16),
        pltpu.VMEM((c, rows, hidden), BF16),
        pltpu.VMEM((c, rows, padded_vocab), F32),
        pltpu.VMEM((c, rows, padded_vocab), BF16),
        pltpu.VMEM((c, rows, 1), F32),
        pltpu.VMEM((c, rows, 1), F32),
        *unit_sum,
        pltpu.VMEM((c, rows, D), BF16),
        pltpu.VMEM((c, 8, 128), F32),
        pltpu.VMEM((c, 15, 8, 128), F32),
        pltpu.VMEM((c, rows, D), BF16),
        pltpu.VMEM((c, rows // 2, D), BF16),
        pltpu.VMEM((c, rows // 2, D), BF16),
        pltpu.VMEM((c, 7, part, D), BF16),
        *unit_sum,
        pltpu.VMEM((c, part, D), F32),
        pltpu.VMEM((c, part, D), F32),
        pltpu.SemaphoreType.DMA((3,)),
        pltpu.SemaphoreType.DMA((160,)),
        pltpu.SemaphoreType.DMA((160,)),
    ]
    vmem = pl.BlockSpec(memory_space=pltpu.VMEM)
    anywhere = pl.BlockSpec(memory_space=pl.ANY)
    result = pl.pallas_call(
        kernel,
        out_shape=jax.ShapeDtypeStruct((block, D), F32),
        in_specs=[vmem, vmem, anywhere, anywhere, vmem, anywhere, vmem, vmem],
        out_specs=vmem,
        scratch_shapes=scratch,
        compiler_params=pltpu.CompilerParams(
            collective_id=0, has_side_effects=True, vmem_limit_bytes=56 * 1024 * 1024
        ),
        cost_estimate=pl.CostEstimate(
            flops=12 * 512 * D * hidden, bytes_accessed=6 * hidden * D, transcendentals=0
        ),
    )(
        x_rows.reshape(block, D), gain_in.reshape(1, D), w_in, w_out, gain_out.reshape(1, D), embed,
        targets, row_mask,
    )
    return result.reshape(1, 1, block, D)


def solution(mesh):
    in_specs = (
        P("vocab", "units", None, None),
        P(),
        P(None, "units"),
        P("units", None),
        P(),
        P("vocab", None),
        P(None, "units", None),
        P(None, "units", None),
    )
    out_specs = P("vocab", "units", None, None)
    return jax.shard_map(local, mesh=mesh, in_specs=in_specs, out_specs=out_specs, check_vma=False)
```

```python
import functools
import math

import jax
import jax.numpy as jnp
from jax import lax
from jax.experimental import pallas as pl
from jax.experimental.pallas import tpu as pltpu
from jax.sharding import PartitionSpec as P

D = 1024
VOCAB = 32128
EPSILON = 1e-06
CHUNKS = 2
TILE = 256
SENDS = 99 * CHUNKS
F32, BF16 = jnp.float32, jnp.bfloat16
MESH = pl.DeviceIdType.MESH
STEPS = (2, 1, 3)
CHIP_STEPS = ((1, 2), (0, 2), (1, 1), (1, 3), (0, 1), (0, 3), (1, 0))
PEER_STEPS = tuple(s + (c,) for s in CHIP_STEPS for c in (0, 1)) + ((0, 0, 1),)
NT = (((1,), (1,)), ((), ()))


def norm_scale(values):
    return lax.rsqrt(jnp.mean(values * values, axis=-1, keepdims=True) + EPSILON)


def norm_back(grad_in, values, scale_rows, gain_vec):
    scaled = grad_in * gain_vec
    inner_sum = jnp.mean(scaled * values, axis=-1, keepdims=True)
    return scaled * scale_rows - values * (scale_rows * scale_rows * scale_rows) * inner_sum


def eye(rows, columns, shift=0):
    row = lax.broadcasted_iota(jnp.int32, (rows, columns), 0)
    return row + shift == lax.broadcasted_iota(jnp.int32, (rows, columns), 1)


def as_row(column):
    return jnp.sum(jnp.where(eye(128, 128), column, 0.0), axis=0, keepdims=True)


def as_column(row, mask):
    return jnp.sum(jnp.where(mask, row, 0.0), axis=1, keepdims=True)


def kernel(
    x_ref, gain_in_ref, w_in_hbm, w_out_hbm, gain_out_ref, embed_hbm, targets_ref, mask_ref,
    out_ref,
    w_in, w_out, embed, near, active, logits, grads, label, weight,
    fwd_all, fwd_part, fwd_own, fwd_x, fwd_mid, fwd_z,
    head_all, stats, stats_in, head_part, head_core, head_mid, head_in,
    bwd_all, bwd_part, bwd_own, bwd_x, bwd_mid, bwd_z,
    summed_ref, grad_sum_ref, local_sem, send_sem, recv_sem,
):
    vocab = lax.axis_index("vocab")
    unit = lax.axis_index("units")
    x_at, z_at = unit // 4, unit % 4
    core, y_at, zlo_at = vocab % 2, (vocab // 2) % 4, vocab // 8
    local_vocab = embed_hbm.shape[0]
    padded_vocab = embed.shape[0]
    block = x_ref.shape[0]
    part = block // CHUNKS
    rows = 16 * part
    hidden = w_in.shape[1]
    factor = 1.0 / math.sqrt(D)
    chunks = range(CHUNKS)

    def unit_peer(dx, dz):
        return vocab, ((x_at + dx) % 4) * 4 + (z_at + dz) % 4

    def vocab_peer(dzlo, dy, dcore):
        return ((zlo_at + dzlo) % 2) * 8 + ((y_at + dy) % 4) * 2 + (core + dcore) % 2, unit

    def chip_slot(dzlo, dy):
        return ((zlo_at + dzlo) % 2) * 4 + (y_at + dy) % 4

    def tiles(size):
        return [slice(start, start + TILE) for start in range(0, size, TILE)]

    def take(start, size):
        return pl.ds(pl.multiple_of(start, size), size)

    used = [0]
    started = []

    def send(src, dst, peer):
        k = used[0]
        used[0] += 1
        copy = pltpu.make_async_remote_copy(
            src_ref=src, dst_ref=dst, send_sem=send_sem.at[k], recv_sem=recv_sem.at[k],
            device_id=peer, device_id_type=MESH,
        )
        copy.start()
        started.append(copy)
        return copy

    loads = [
        pltpu.make_async_copy(w_in_hbm, w_in, local_sem.at[0]),
        pltpu.make_async_copy(w_out_hbm, w_out, local_sem.at[1]),
        pltpu.make_async_copy(embed_hbm, embed.at[pl.ds(0, local_vocab)], local_sem.at[2]),
    ]
    for load in loads:
        load.start()

    barrier = pltpu.get_barrier_semaphore()
    greet = [unit_peer(d, 0) for d in STEPS] + [unit_peer(0, d) for d in STEPS]
    greet += [vocab_peer(*s) for s in PEER_STEPS]
    for peer in greet:
        pl.semaphore_signal(barrier, inc=1, device_id=peer, device_id_type=MESH)

    inputs = x_ref[...].astype(F32)
    scale_in = norm_scale(inputs)
    normed = (inputs * scale_in * gain_in_ref[...]).astype(BF16)
    for c in chunks:
        fwd_all[c, 0:part, :] = normed[c * part : (c + 1) * part]
    embed[local_vocab:, :] = jnp.zeros((padded_vocab - local_vocab, D), BF16)
    pl.semaphore_wait(barrier, len(greet))

    def unit_gather_start(buf):
        along_z = [
            send(buf.at[pl.ds(0, part)], buf.at[pl.ds((4 - d) * part, part)], unit_peer(0, d))
            for d in STEPS
        ]
        along_x = [
            send(buf.at[pl.ds(0, part)], buf.at[pl.ds((4 - d) * 4 * part, part)], unit_peer(d, 0))
            for d in STEPS
        ]
        return along_z, along_x

    def unit_gather_pass(buf, along_z, along_x, which):
        for k in which:
            along_z[k].wait_recv()
            dz = 4 - STEPS[k]
            along_x += [
                send(
                    buf.at[pl.ds(dz * part, part)],
                    buf.at[pl.ds(((4 - d) * 4 + dz) * part, part)],
                    unit_peer(d, 0),
                )
                for d in STEPS
            ]

    def unit_sum_start(partial, landing):
        return [
            [
                send(
                    partial.at[pl.ds((d * 4 + dz) * part, part)],
                    landing.at[d - 1, pl.ds(dz * part, part)],
                    unit_peer(d, 0),
                )
                for d in STEPS
            ]
            for dz in STEPS + (0,)
        ]

    def unit_sum_pass(copies, own, landing, mid, landing_z):
        along_z = []
        for dz, arrivals in zip(STEPS + (0,), copies):
            for copy in arrivals:
                copy.wait_recv()
            at = slice(dz * part, (dz + 1) * part)
            total = own[at, :]
            for d in (1, 2, 3):
                total = total + landing[d - 1, at, :].astype(F32)
            if dz:
                mid[at, :] = total.astype(BF16)
                along_z.append(
                    send(mid.at[pl.ds(dz * part, part)], landing_z.at[dz - 1], unit_peer(0, dz))
                )
            else:
                own[at, :] = total
        return along_z

    def unit_sum_end(copies, own, landing_z):
        for copy in copies:
            copy.wait_recv()
        total = own[0:part, :]
        for d in (1, 2, 3):
            total = total + landing_z[d - 1].astype(F32)
        return total

    fwd = [unit_gather_start(fwd_all.at[c]) for c in chunks]

    for c in chunks:
        pick = eye(part, block, c * part)
        for slot in range(16):
            owner = ((slot // 4) % 2) * 8 + (slot % 4) * 2 + slot // 8
            label[c, slot * part : (slot + 1) * part, :] = as_column(
                targets_ref[owner].astype(F32), pick
            )
            weight[c, slot * part : (slot + 1) * part, :] = as_column(
                mask_ref[owner].astype(F32), pick
            )

    for which in ((1, 2), (0,)):
        for c in chunks:
            unit_gather_pass(fwd_all.at[c], *fwd[c], which)

    fwd_sum = []
    for c in chunks:
        if c == 0:
            loads[0].wait()
        for copy in fwd[c][1]:
            copy.wait_recv()

        for at in tiles(hidden):
            before = jnp.dot(fwd_all[c], w_in[:, at], preferred_element_type=F32)
            active[c, :, at] = jnp.maximum(before, 0.0).astype(BF16)

        if c == 0:
            loads[1].wait()

        for at in tiles(D):
            product = jnp.dot(active[c], w_out[:, at], preferred_element_type=F32)
            fwd_own[c, :, at] = product[0 : 4 * part]
            fwd_part[c, :, at] = product.astype(BF16)

        fwd_sum.append(unit_sum_start(fwd_part.at[c], fwd_x.at[c]))

    fwd_sum = [
        unit_sum_pass(fwd_sum[c], fwd_own.at[c], fwd_x.at[c], fwd_mid.at[c], fwd_z.at[c])
        for c in chunks
    ]

    my_slot = core * 8 + chip_slot(0, 0)
    head = []
    for c in chunks:
        summed = inputs[c * part : (c + 1) * part] + unit_sum_end(
            fwd_sum[c], fwd_own.at[c], fwd_z.at[c]
        )
        summed_ref[c] = summed
        final = (summed * norm_scale(summed) * gain_out_ref[...]).astype(BF16)
        mine = head_all.at[c, take(my_slot * part, part)]
        mine[...] = final
        head.append([send(mine, mine, vocab_peer(*s, 0)) for s in CHIP_STEPS])
        head[c].append(send(mine, mine, vocab_peer(0, 0, 1)))

    loads[2].wait()
    lane = lax.broadcasted_iota(jnp.int32, (1, TILE), 1)
    exchange = []
    top = []
    for c in chunks:
        across = [head[c][-1]]
        for copy, (dzlo, dy) in reversed(list(zip(head[c][:-1], CHIP_STEPS))):
            copy.wait_recv()
            slot = head_all.at[c, take((core * 8 + chip_slot(-dzlo, -dy)) * part, part)]
            across.append(send(slot, slot, vocab_peer(0, 0, 1)))
        for copy in across:
            copy.wait_recv()

        best = jnp.full((rows, 128), -1e30, F32)
        for at in tiles(padded_vocab):
            tile = lax.dot_general(head_all[c], embed[at, :], NT, preferred_element_type=F32)
            here = lane + at.start
            live = jnp.logical_and(here < local_vocab, here + vocab * local_vocab < VOCAB)
            tile = jnp.where(live, tile * factor, -1e30)
            logits[c, :, at] = tile
            for k in range(TILE // 128):
                best = jnp.maximum(best, tile[:, k * 128 : (k + 1) * 128])
        local_top = jnp.max(best, axis=1, keepdims=True)

        acc = jnp.zeros((rows, 128), F32)
        for at in tiles(padded_vocab):
            tile = jnp.exp(logits[c, :, at] - local_top)
            logits[c, :, at] = tile
            for k in range(TILE // 128):
                acc = acc + tile[:, k * 128 : (k + 1) * 128]
        local_sum = jnp.sum(acc, axis=1, keepdims=True)
        halves = rows // 128
        stats[c] = jnp.zeros((8, 128), F32)
        for h in range(halves):
            stats[c, h : h + 1, :] = as_row(local_top[h * 128 : (h + 1) * 128])
            stats[c, 4 + h : 5 + h, :] = as_row(local_sum[h * 128 : (h + 1) * 128])
        exchange.append(
            [send(stats.at[c], stats_in.at[c, k], vocab_peer(*s)) for k, s in enumerate(PEER_STEPS)]
        )

    head_sum = []
    for c in chunks:
        for copy in exchange[c]:
            copy.wait_recv()
        own_top, own_sum = stats[c, 0:4, :], stats[c, 4:8, :]
        row_top = own_top
        for k in range(len(PEER_STEPS)):
            row_top = jnp.maximum(row_top, stats_in[c, k, 0:4, :])
        row_sum = own_sum * jnp.exp(own_top - row_top)
        for k in range(len(PEER_STEPS)):
            row_sum = row_sum + stats_in[c, k, 4:8, :] * jnp.exp(stats_in[c, k, 0:4, :] - row_top)
        ratio_rows = jnp.exp(own_top - row_top) / row_sum
        ratio = jnp.concatenate(
            [as_column(ratio_rows[h : h + 1], eye(128, 128)) for h in range(rows // 128)], axis=0
        )
        wanted = label[c].astype(jnp.int32) - vocab * local_vocab

        for at in tiles(padded_vocab):
            onehot = (lane + at.start == wanted).astype(F32)
            grads[c, :, at] = (weight[c] * (logits[c, :, at] * ratio - onehot)).astype(BF16)

        half = rows // 2
        across = []
        for at in tiles(D):
            product = jnp.dot(grads[c], embed[:, at], preferred_element_type=F32) * factor
            head_part[c, :, at] = product.astype(BF16)
            if at.stop % 512 == 0:
                columns = pl.ds(at.stop - 512, 512)
                across.append(
                    send(
                        head_part.at[c, take((1 - core) * half, half), columns],
                        head_core.at[c, :, columns], vocab_peer(0, 0, 1),
                    )
                )
        head_sum.append(across)

    for c in chunks:
        for copy in head_sum[c]:
            copy.wait_recv()
        half = rows // 2
        total = head_part[c, take(core * half, half), :].astype(F32) + head_core[c].astype(F32)
        head_mid[c] = total.astype(BF16)
        head_sum[c] = [
            send(
                head_mid.at[c, take(chip_slot(*s) * part, part)], head_in.at[c, k],
                vocab_peer(*s, 0),
            )
            for k, s in enumerate(CHIP_STEPS)
        ]

    bwd = []
    for c in chunks:
        for copy in head_sum[c]:
            copy.wait_recv()
        grad_final = head_mid[c, take(chip_slot(0, 0) * part, part), :].astype(F32)
        for k in range(len(CHIP_STEPS)):
            grad_final = grad_final + head_in[c, k].astype(F32)
        summed = summed_ref[c]
        grad_sum = norm_back(grad_final, summed, norm_scale(summed), gain_out_ref[...])
        grad_sum_ref[c] = grad_sum
        bwd_all[c, 0:part, :] = grad_sum.astype(BF16)
        bwd.append(unit_gather_start(bwd_all.at[c]))
    for which in ((1, 2), (0,)):
        for c in chunks:
            unit_gather_pass(bwd_all.at[c], *bwd[c], which)

    bwd_sum = []
    for c in chunks:
        for copy in bwd[c][1]:
            copy.wait_recv()

        for at in tiles(hidden):
            product = lax.dot_general(bwd_all[c], w_out[at, :], NT, preferred_element_type=F32)
            held = active[c, :, at]
            near[c, :, at] = jnp.where(held.astype(F32) > 0.0, product, 0.0).astype(BF16)

        for at in tiles(D):
            product = lax.dot_general(near[c], w_in[at, :], NT, preferred_element_type=F32)
            bwd_own[c, :, at] = product[0 : 4 * part]
            bwd_part[c, :, at] = product.astype(BF16)

        bwd_sum.append(unit_sum_start(bwd_part.at[c], bwd_x.at[c]))

    bwd_sum = [
        unit_sum_pass(bwd_sum[c], bwd_own.at[c], bwd_x.at[c], bwd_mid.at[c], bwd_z.at[c])
        for c in chunks
    ]
    for c in chunks:
        grad_normed = unit_sum_end(bwd_sum[c], bwd_own.at[c], bwd_z.at[c])
        here = slice(c * part, (c + 1) * part)
        out_ref[here, :] = grad_sum_ref[c] + norm_back(
            grad_normed, inputs[here], scale_in[here], gain_in_ref[...]
        )
    assert len(started) == SENDS
    for copy in started:
        copy.wait_send()


def local(x_rows, gain_in, w_in, w_out, gain_out, embed, targets, row_mask):
    block = x_rows.shape[2]
    part = block // CHUNKS
    rows = 16 * part
    hidden = w_in.shape[1]
    padded_vocab = (embed.shape[0] + 511) // 512 * 512
    c = CHUNKS
    unit_sum = [
        pltpu.VMEM((c, rows, D), BF16),
        pltpu.VMEM((c, rows, D), BF16),
        pltpu.VMEM((c, 4 * part, D), F32),
        pltpu.VMEM((c, 3, 4 * part, D), BF16),
        pltpu.VMEM((c, 4 * part, D), BF16),
        pltpu.VMEM((c, 3, part, D), BF16),
    ]
    scratch = [
        pltpu.VMEM(w_in.shape, BF16),
        pltpu.VMEM(w_out.shape, BF16),
        pltpu.VMEM((padded_vocab, D), BF16),
        pltpu.VMEM((c, rows, hidden), BF16),
        pltpu.VMEM((c, rows, hidden), BF16),
        pltpu.VMEM((c, rows, padded_vocab), F32),
        pltpu.VMEM((c, rows, padded_vocab), BF16),
        pltpu.VMEM((c, rows, 1), F32),
        pltpu.VMEM((c, rows, 1), F32),
        *unit_sum,
        pltpu.VMEM((c, rows, D), BF16),
        pltpu.VMEM((c, 8, 128), F32),
        pltpu.VMEM((c, 15, 8, 128), F32),
        pltpu.VMEM((c, rows, D), BF16),
        pltpu.VMEM((c, rows // 2, D), BF16),
        pltpu.VMEM((c, rows // 2, D), BF16),
        pltpu.VMEM((c, 7, part, D), BF16),
        *unit_sum,
        pltpu.VMEM((c, part, D), F32),
        pltpu.VMEM((c, part, D), F32),
        pltpu.SemaphoreType.DMA((3,)),
        pltpu.SemaphoreType.DMA((SENDS,)),
        pltpu.SemaphoreType.DMA((SENDS,)),
    ]
    vmem = pl.BlockSpec(memory_space=pltpu.VMEM)
    anywhere = pl.BlockSpec(memory_space=pl.ANY)
    result = pl.pallas_call(
        kernel,
        out_shape=jax.ShapeDtypeStruct((block, D), F32),
        in_specs=[vmem, vmem, anywhere, anywhere, vmem, anywhere, vmem, vmem],
        out_specs=vmem,
        scratch_shapes=scratch,
        compiler_params=pltpu.CompilerParams(
            collective_id=0, has_side_effects=True, vmem_limit_bytes=56 * 1024 * 1024
        ),
        cost_estimate=pl.CostEstimate(
            flops=12 * 512 * D * hidden, bytes_accessed=6 * hidden * D, transcendentals=0
        ),
    )(
        x_rows.reshape(block, D), gain_in.reshape(1, D), w_in, w_out, gain_out.reshape(1, D), embed,
        targets, row_mask,
    )
    return result.reshape(1, 1, block, D)


def solution(mesh):
    in_specs = (
        P("vocab", "units", None, None),
        P(),
        P(None, "units"),
        P("units", None),
        P(),
        P("vocab", None),
        P(None, "units", None),
        P(None, "units", None),
    )
    out_specs = P("vocab", "units", None, None)
    return jax.shard_map(local, mesh=mesh, in_specs=in_specs, out_specs=out_specs, check_vma=False)
```

```python
import functools
import math

import jax
import jax.numpy as jnp
from jax import lax
from jax.experimental import pallas as pl
from jax.experimental.pallas import tpu as pltpu
from jax.sharding import PartitionSpec as P

D = 1024
VOCAB = 32128
EPSILON = 1e-06
CHUNKS = 2
TILE = 256
SENDS = 113 * CHUNKS
ORDER = [int(c) for c in "0101010100011101010101010101010100011101"]
F32, BF16 = jnp.float32, jnp.bfloat16
MESH = pl.DeviceIdType.MESH
STEPS = (2, 1, 3)
NEAR, SIDE, FAR = 1, 2, 3
Z_STEPS = (FAR, SIDE, NEAR)
SPLIT = 256
EVERY, DIRECT, TURNED = pl.ds(0, D), pl.ds(0, SPLIT), pl.ds(SPLIT, D - SPLIT)
CHIP_STEPS = ((1, 2), (0, 2), (1, 1), (1, 3), (0, 1), (0, 3), (1, 0))
PEER_STEPS = tuple(s + (c,) for s in CHIP_STEPS for c in (0, 1)) + ((0, 0, 1),)
NT = (((1,), (1,)), ((), ()))


def norm_scale(values):
    return lax.rsqrt(jnp.mean(values * values, axis=-1, keepdims=True) + EPSILON)


def norm_back(grad_in, values, scale_rows, gain_vec):
    scaled = grad_in * gain_vec
    inner_sum = jnp.mean(scaled * values, axis=-1, keepdims=True)
    return scaled * scale_rows - values * (scale_rows * scale_rows * scale_rows) * inner_sum


def eye(rows, columns, shift=0):
    row = lax.broadcasted_iota(jnp.int32, (rows, columns), 0)
    return row + shift == lax.broadcasted_iota(jnp.int32, (rows, columns), 1)


def as_row(column):
    return jnp.sum(jnp.where(eye(128, 128), column, 0.0), axis=0, keepdims=True)


def as_column(row, mask):
    return jnp.sum(jnp.where(mask, row, 0.0), axis=1, keepdims=True)


def kernel(
    x_ref, gain_in_ref, w_in_hbm, w_out_hbm, gain_out_ref, embed_hbm, targets_ref, mask_ref,
    out_ref,
    w_in, w_out, embed, near, active, logits, grads, label, weight,
    fwd_all, fwd_part, fwd_own, fwd_x, fwd_mid, fwd_z, fwd_turn, fwd_turn_mid, fwd_turn_in,
    head_all, stats, stats_in, head_part, head_core, head_mid, head_in,
    bwd_all, bwd_part, bwd_own, bwd_x, bwd_mid, bwd_z, bwd_turn, bwd_turn_mid, bwd_turn_in,
    summed_ref, grad_sum_ref, local_sem, send_sem, recv_sem,
):
    vocab = lax.axis_index("vocab")
    unit = lax.axis_index("units")
    x_at, z_at = unit // 4, unit % 4
    core, y_at, zlo_at = vocab % 2, (vocab // 2) % 4, vocab // 8
    local_vocab = embed_hbm.shape[0]
    padded_vocab = embed.shape[0]
    block = x_ref.shape[0]
    part = block // CHUNKS
    rows = 16 * part
    hidden = w_in.shape[1]
    factor = 1.0 / math.sqrt(D)
    chunks = range(CHUNKS)

    def x_peer(dx):
        return vocab, ((x_at + dx) % 4) * 4 + z_at

    towards = 2 * zlo_at - 1

    def z_chip(z_hi, z_lo):
        return z_lo * 8 + y_at * 2 + core, x_at * 4 + z_hi % 4

    def z_peer(k):
        if k == SIDE:
            return z_chip(z_at + 4 - towards, zlo_at)
        return z_chip(z_at + (4 + towards if k == NEAR else 2), 1 - zlo_at)

    def z_source(k):
        return z_chip(z_at + 4 + towards, zlo_at) if k == SIDE else z_peer(k)

    def vocab_peer(dzlo, dy, dcore):
        return ((zlo_at + dzlo) % 2) * 8 + ((y_at + dy) % 4) * 2 + (core + dcore) % 2, unit

    def chip_slot(dzlo, dy):
        return ((zlo_at + dzlo) % 2) * 4 + (y_at + dy) % 4

    def tiles(size):
        return [slice(start, start + TILE) for start in range(0, size, TILE)]

    def take(start, size):
        return pl.ds(pl.multiple_of(start, size), size)

    used = [0]
    started = []

    def send(src, dst, peer):
        k = used[0]
        used[0] += 1
        copy = pltpu.make_async_remote_copy(
            src_ref=src, dst_ref=dst, send_sem=send_sem.at[k], recv_sem=recv_sem.at[k],
            device_id=peer, device_id_type=MESH,
        )
        copy.start()
        started.append(copy)
        return copy

    loads = [
        pltpu.make_async_copy(w_in_hbm, w_in, local_sem.at[0]),
        pltpu.make_async_copy(w_out_hbm, w_out, local_sem.at[1]),
        pltpu.make_async_copy(embed_hbm, embed.at[pl.ds(0, local_vocab)], local_sem.at[2]),
    ]
    for load in loads:
        load.start()

    barrier = pltpu.get_barrier_semaphore()
    greet = [x_peer(d) for d in STEPS] + [z_peer(k) for k in Z_STEPS] + [z_source(SIDE)]
    greet += [vocab_peer(*s) for s in PEER_STEPS]
    for peer in greet:
        pl.semaphore_signal(barrier, inc=1, device_id=peer, device_id_type=MESH)

    inputs = x_ref[...].astype(F32)
    scale_in = norm_scale(inputs)
    normed = (inputs * scale_in * gain_in_ref[...]).astype(BF16)
    for c in chunks:
        fwd_all[c, 0:part, :] = normed[c * part : (c + 1) * part]
    embed[local_vocab:, :] = jnp.zeros((padded_vocab - local_vocab, D), BF16)
    pl.semaphore_wait(barrier, len(greet))

    my_slot = core * 8 + chip_slot(0, 0)

    def unit_gather(buf):
        def block(dx, k, columns=EVERY):
            return buf.at[pl.ds((dx * 4 + k) * part, part), columns]

        along_z = [send(block(0, 0), block(0, k), z_peer(k)) for k in Z_STEPS]
        along_x = [send(block(0, 0), block(4 - d, 0), x_peer(d)) for d in STEPS]
        across = along_x[:1]
        landed = along_x[1:]
        for k, copy in reversed(list(zip(Z_STEPS, along_z))):
            if k != SIDE:
                yield
            copy.wait_recv()
            for d in STEPS:
                columns = DIRECT if d == 2 else EVERY
                landed.append(send(block(0, k, columns), block(4 - d, k, columns), x_peer(d)))
            if k == NEAR:
                across[0].wait_recv()
                landed += [
                    send(block(2, 0, TURNED), block(2, m, TURNED), z_peer(m)) for m in Z_STEPS
                ]
        yield
        for copy in landed:
            copy.wait_recv()

    def unit_sum(partial, own, landing, mid, landing_z, turn, turn_mid, turn_in):
        def block(dx, k, columns=EVERY):
            return partial.at[pl.ds((dx * 4 + k) * part, part), columns]

        def rows_of(k):
            return slice(k * part, (k + 1) * part)

        turning = [send(block(2, k, TURNED), turn.at[k - 1], z_source(k)) for k in Z_STEPS]
        along_x = {}
        for k in Z_STEPS + (0,):
            along_x[k] = []
            for d in STEPS:
                columns = DIRECT if d == 2 else EVERY
                to = landing.at[d - 1, pl.ds(k * part, part), columns]
                along_x[k].append(send(block(d, k, columns), to, x_peer(d)))
        along_z = []
        for k in Z_STEPS + (0,):
            if k != NEAR:
                yield
            if k == SIDE:
                for copy in turning:
                    copy.wait_recv()
                total = partial[8 * part : 9 * part, SPLIT:].astype(F32)
                for m in range(3):
                    total = total + turn[m].astype(F32)
                turn_mid[...] = total.astype(BF16)
                turned = send(turn_mid, turn_in, x_peer(2))
            for copy in along_x[k]:
                copy.wait_recv()
            at = rows_of(k)
            total = own[at, :] + landing[0, at, :].astype(F32) + landing[2, at, :].astype(F32)
            direct = total[:, :SPLIT] + landing[1, at, :SPLIT].astype(F32)
            if k:
                mid[at, :SPLIT] = direct.astype(BF16)
                mid[at, SPLIT:] = total[:, SPLIT:].astype(BF16)
                along_z.append(send(mid.at[pl.ds(k * part, part)], landing_z.at[k - 1], z_source(k)))
        yield
        for copy in along_z + [turned]:
            copy.wait_recv()
        total = jnp.concatenate([direct, total[:, SPLIT:] + turn_in[...].astype(F32)], axis=1)
        for m in range(3):
            total = total + landing_z[m].astype(F32)
        return total

    lane = lax.broadcasted_iota(jnp.int32, (1, TILE), 1)
    half = rows // 2

    def chain(c):
        here = slice(c * part, (c + 1) * part)
        gather = unit_gather(fwd_all.at[c])
        next(gather)
        yield

        pick = eye(part, block, c * part)
        for slot in range(16):
            owner = ((slot // 4) % 2) * 8 + (slot % 4) * 2 + slot // 8
            at = slice(slot * part, (slot + 1) * part)
            label[c, at, :] = as_column(targets_ref[owner].astype(F32), pick)
            weight[c, at, :] = as_column(mask_ref[owner].astype(F32), pick)
        yield from gather

        if c == 0:
            loads[0].wait()
        for at in tiles(hidden):
            before = jnp.dot(fwd_all[c], w_in[:, at], preferred_element_type=F32)
            active[c, :, at] = jnp.maximum(before, 0.0).astype(BF16)
        if c == 0:
            loads[1].wait()
        for at in tiles(D):
            product = jnp.dot(active[c], w_out[:, at], preferred_element_type=F32)
            fwd_own[c, :, at] = product[0 : 4 * part]
            fwd_part[c, :, at] = product.astype(BF16)
        branch = yield from unit_sum(
            fwd_part.at[c], fwd_own.at[c], fwd_x.at[c], fwd_mid.at[c], fwd_z.at[c],
            fwd_turn.at[c], fwd_turn_mid.at[c], fwd_turn_in.at[c]
        )

        summed = inputs[here] + branch
        scale_out = norm_scale(summed)
        summed_ref[c] = summed
        mine = head_all.at[c, take(my_slot * part, part)]
        mine[...] = (summed * scale_out * gain_out_ref[...]).astype(BF16)
        arrivals = [send(mine, mine, vocab_peer(*s, 0)) for s in CHIP_STEPS]
        across = [send(mine, mine, vocab_peer(0, 0, 1))]
        yield
        for copy, (dzlo, dy) in reversed(list(zip(arrivals, CHIP_STEPS))):
            copy.wait_recv()
            slot = head_all.at[c, take((core * 8 + chip_slot(-dzlo, -dy)) * part, part)]
            across.append(send(slot, slot, vocab_peer(0, 0, 1)))
        yield
        for copy in across:
            copy.wait_recv()

        if c == 0:
            loads[2].wait()
        best = jnp.full((rows, 128), -1e30, F32)
        for at in tiles(padded_vocab):
            tile = lax.dot_general(head_all[c], embed[at, :], NT, preferred_element_type=F32)
            column = lane + at.start
            live = jnp.logical_and(column < local_vocab, column + vocab * local_vocab < VOCAB)
            tile = jnp.where(live, tile * factor, -1e30)
            logits[c, :, at] = tile
            for k in range(TILE // 128):
                best = jnp.maximum(best, tile[:, k * 128 : (k + 1) * 128])
        local_top = jnp.max(best, axis=1, keepdims=True)
        acc = jnp.zeros((rows, 128), F32)
        for at in tiles(padded_vocab):
            tile = jnp.exp(logits[c, :, at] - local_top)
            logits[c, :, at] = tile
            for k in range(TILE // 128):
                acc = acc + tile[:, k * 128 : (k + 1) * 128]
        local_sum = jnp.sum(acc, axis=1, keepdims=True)
        stats[c] = jnp.zeros((8, 128), F32)
        for h in range(rows // 128):
            stats[c, h : h + 1, :] = as_row(local_top[h * 128 : (h + 1) * 128])
            stats[c, 4 + h : 5 + h, :] = as_row(local_sum[h * 128 : (h + 1) * 128])
        exchange = [
            send(stats.at[c], stats_in.at[c, k], vocab_peer(*s)) for k, s in enumerate(PEER_STEPS)
        ]
        yield
        for copy in exchange:
            copy.wait_recv()

        own_top, own_sum = stats[c, 0:4, :], stats[c, 4:8, :]
        row_top = own_top
        for k in range(len(PEER_STEPS)):
            row_top = jnp.maximum(row_top, stats_in[c, k, 0:4, :])
        row_sum = own_sum * jnp.exp(own_top - row_top)
        for k in range(len(PEER_STEPS)):
            row_sum = row_sum + stats_in[c, k, 4:8, :] * jnp.exp(stats_in[c, k, 0:4, :] - row_top)
        ratio_rows = jnp.exp(own_top - row_top) / row_sum
        ratio = jnp.concatenate(
            [as_column(ratio_rows[h : h + 1], eye(128, 128)) for h in range(rows // 128)], axis=0
        )
        wanted = label[c].astype(jnp.int32) - vocab * local_vocab
        for at in tiles(padded_vocab):
            onehot = (lane + at.start == wanted).astype(F32)
            grads[c, :, at] = (weight[c] * (logits[c, :, at] * ratio - onehot)).astype(BF16)
        across = []
        for at in tiles(D):
            product = jnp.dot(grads[c], embed[:, at], preferred_element_type=F32) * factor
            head_part[c, :, at] = product.astype(BF16)
            if at.stop % 512 == 0:
                columns = pl.ds(at.stop - 512, 512)
                across.append(
                    send(
                        head_part.at[c, take((1 - core) * half, half), columns],
                        head_core.at[c, :, columns], vocab_peer(0, 0, 1),
                    )
                )
        yield
        for copy in across:
            copy.wait_recv()

        total = head_part[c, take(core * half, half), :].astype(F32) + head_core[c].astype(F32)
        head_mid[c] = total.astype(BF16)
        arrivals = [
            send(
                head_mid.at[c, take(chip_slot(*s) * part, part)], head_in.at[c, k],
                vocab_peer(*s, 0),
            )
            for k, s in enumerate(CHIP_STEPS)
        ]
        yield
        for copy in arrivals:
            copy.wait_recv()

        grad_final = head_mid[c, take(chip_slot(0, 0) * part, part), :].astype(F32)
        for k in range(len(CHIP_STEPS)):
            grad_final = grad_final + head_in[c, k].astype(F32)
        summed = summed_ref[c]
        grad_sum = norm_back(grad_final, summed, norm_scale(summed), gain_out_ref[...])
        grad_sum_ref[c] = grad_sum
        bwd_all[c, 0:part, :] = grad_sum.astype(BF16)
        yield from unit_gather(bwd_all.at[c])

        for at in tiles(hidden):
            product = lax.dot_general(bwd_all[c], w_out[at, :], NT, preferred_element_type=F32)
            held = active[c, :, at].astype(F32)
            near[c, :, at] = jnp.where(held > 0.0, product, 0.0).astype(BF16)
        for at in tiles(D):
            product = lax.dot_general(near[c], w_in[at, :], NT, preferred_element_type=F32)
            bwd_own[c, :, at] = product[0 : 4 * part]
            bwd_part[c, :, at] = product.astype(BF16)
        grad_normed = yield from unit_sum(
            bwd_part.at[c], bwd_own.at[c], bwd_x.at[c], bwd_mid.at[c], bwd_z.at[c],
            bwd_turn.at[c], bwd_turn_mid.at[c], bwd_turn_in.at[c]
        )
        out_ref[here, :] = grad_sum_ref[c] + norm_back(
            grad_normed, inputs[here], scale_in[here], gain_in_ref[...]
        )

    chains = [chain(c) for c in chunks]
    for c in ORDER:
        next(chains[c], None)
    assert len(started) == SENDS
    for copy in started:
        copy.wait_send()


def local(x_rows, gain_in, w_in, w_out, gain_out, embed, targets, row_mask):
    block = x_rows.shape[2]
    part = block // CHUNKS
    rows = 16 * part
    hidden = w_in.shape[1]
    padded_vocab = (embed.shape[0] + 511) // 512 * 512
    c = CHUNKS
    unit_sum = [
        pltpu.VMEM((c, rows, D), BF16),
        pltpu.VMEM((c, rows, D), BF16),
        pltpu.VMEM((c, 4 * part, D), F32),
        pltpu.VMEM((c, 3, 4 * part, D), BF16),
        pltpu.VMEM((c, 4 * part, D), BF16),
        pltpu.VMEM((c, 3, part, D), BF16),
        pltpu.VMEM((c, 3, part, D - SPLIT), BF16),
        pltpu.VMEM((c, part, D - SPLIT), BF16),
        pltpu.VMEM((c, part, D - SPLIT), BF16),
    ]
    scratch = [
        pltpu.VMEM(w_in.shape, BF16),
        pltpu.VMEM(w_out.shape, BF16),
        pltpu.VMEM((padded_vocab, D), BF16),
        pltpu.VMEM((c, rows, hidden), BF16),
        pltpu.VMEM((c, rows, hidden), BF16),
        pltpu.VMEM((c, rows, padded_vocab), F32),
        pltpu.VMEM((c, rows, padded_vocab), BF16),
        pltpu.VMEM((c, rows, 1), F32),
        pltpu.VMEM((c, rows, 1), F32),
        *unit_sum,
        pltpu.VMEM((c, rows, D), BF16),
        pltpu.VMEM((c, 8, 128), F32),
        pltpu.VMEM((c, 15, 8, 128), F32),
        pltpu.VMEM((c, rows, D), BF16),
        pltpu.VMEM((c, rows // 2, D), BF16),
        pltpu.VMEM((c, rows // 2, D), BF16),
        pltpu.VMEM((c, 7, part, D), BF16),
        *unit_sum,
        pltpu.VMEM((c, part, D), F32),
        pltpu.VMEM((c, part, D), F32),
        pltpu.SemaphoreType.DMA((3,)),
        pltpu.SemaphoreType.DMA((SENDS,)),
        pltpu.SemaphoreType.DMA((SENDS,)),
    ]
    vmem = pl.BlockSpec(memory_space=pltpu.VMEM)
    anywhere = pl.BlockSpec(memory_space=pl.ANY)
    result = pl.pallas_call(
        kernel,
        out_shape=jax.ShapeDtypeStruct((block, D), F32),
        in_specs=[vmem, vmem, anywhere, anywhere, vmem, anywhere, vmem, vmem],
        out_specs=vmem,
        scratch_shapes=scratch,
        compiler_params=pltpu.CompilerParams(
            collective_id=0, has_side_effects=True, vmem_limit_bytes=56 * 1024 * 1024
        ),
        cost_estimate=pl.CostEstimate(
            flops=12 * 512 * D * hidden, bytes_accessed=6 * hidden * D, transcendentals=0
        ),
    )(
        x_rows.reshape(block, D), gain_in.reshape(1, D), w_in, w_out, gain_out.reshape(1, D), embed,
        targets, row_mask,
    )
    return result.reshape(1, 1, block, D)


def solution(mesh):
    in_specs = (
        P("vocab", "units", None, None),
        P(),
        P(None, "units"),
        P("units", None),
        P(),
        P("vocab", None),
        P(None, "units", None),
        P(None, "units", None),
    )
    out_specs = P("vocab", "units", None, None)
    return jax.shard_map(local, mesh=mesh, in_specs=in_specs, out_specs=out_specs, check_vma=False)
```

```python
import functools
import math

import jax
import jax.numpy as jnp
from jax import lax
from jax.experimental import pallas as pl
from jax.experimental.pallas import tpu as pltpu
from jax.sharding import PartitionSpec as P

D = 1024
VOCAB = 32128
EPSILON = 1e-06
CHUNKS = 2
TILE = 256
SENDS = 113 * CHUNKS
ORDER = [int(c) for c in "0100110100011101010101010100110100011101"]
F32, BF16 = jnp.float32, jnp.bfloat16
MESH = pl.DeviceIdType.MESH
STEPS = (2, 1, 3)
NEAR, SIDE, FAR = 1, 2, 3
Z_STEPS = (FAR, SIDE, NEAR)
SPLIT = 256
EVERY, DIRECT, TURNED = pl.ds(0, D), pl.ds(0, SPLIT), pl.ds(SPLIT, D - SPLIT)
CHIP_STEPS = ((1, 2), (0, 2), (1, 1), (1, 3), (0, 1), (0, 3), (1, 0))
PEER_STEPS = tuple(s + (c,) for s in CHIP_STEPS for c in (0, 1)) + ((0, 0, 1),)
NT = (((1,), (1,)), ((), ()))


def norm_scale(values):
    return lax.rsqrt(jnp.mean(values * values, axis=-1, keepdims=True) + EPSILON)


def norm_back(grad_in, values, scale_rows, gain_vec):
    scaled = grad_in * gain_vec
    inner_sum = jnp.mean(scaled * values, axis=-1, keepdims=True)
    return scaled * scale_rows - values * (scale_rows * scale_rows * scale_rows) * inner_sum


def eye(rows, columns, shift=0):
    row = lax.broadcasted_iota(jnp.int32, (rows, columns), 0)
    return row + shift == lax.broadcasted_iota(jnp.int32, (rows, columns), 1)


def as_row(column):
    return jnp.sum(jnp.where(eye(128, 128), column, 0.0), axis=0, keepdims=True)


def as_column(row, mask):
    return jnp.sum(jnp.where(mask, row, 0.0), axis=1, keepdims=True)


def kernel(
    x_ref, gain_in_ref, w_in_hbm, w_out_hbm, gain_out_ref, embed_hbm, targets_ref, mask_ref,
    out_ref,
    w_in, w_out, embed, near, active, logits, grads, label, weight,
    fwd_all, fwd_part, fwd_own, fwd_x, fwd_mid, fwd_z, fwd_turn, fwd_turn_mid, fwd_turn_in,
    head_all, stats, stats_in, head_part, head_core, head_mid, head_in,
    bwd_all, bwd_part, bwd_own, bwd_x, bwd_mid, bwd_z, bwd_turn, bwd_turn_mid, bwd_turn_in,
    summed_ref, grad_sum_ref, local_sem, send_sem, recv_sem,
):
    vocab = lax.axis_index("vocab")
    unit = lax.axis_index("units")
    x_at, z_at = unit // 4, unit % 4
    core, y_at, zlo_at = vocab % 2, (vocab // 2) % 4, vocab // 8
    local_vocab = embed_hbm.shape[0]
    padded_vocab = embed.shape[0]
    block = x_ref.shape[0]
    part = block // CHUNKS
    rows = 16 * part
    hidden = w_in.shape[1]
    factor = 1.0 / math.sqrt(D)
    chunks = range(CHUNKS)

    def x_peer(dx):
        return vocab, ((x_at + dx) % 4) * 4 + z_at

    towards = 2 * zlo_at - 1

    def z_chip(z_hi, z_lo):
        return z_lo * 8 + y_at * 2 + core, x_at * 4 + z_hi % 4

    def z_peer(k):
        if k == SIDE:
            return z_chip(z_at + 4 - towards, zlo_at)
        return z_chip(z_at + (4 + towards if k == NEAR else 2), 1 - zlo_at)

    def z_source(k):
        return z_chip(z_at + 4 + towards, zlo_at) if k == SIDE else z_peer(k)

    def vocab_peer(dzlo, dy, dcore):
        return ((zlo_at + dzlo) % 2) * 8 + ((y_at + dy) % 4) * 2 + (core + dcore) % 2, unit

    def chip_slot(dzlo, dy):
        return ((zlo_at + dzlo) % 2) * 4 + (y_at + dy) % 4

    def tiles(size):
        return [slice(start, start + TILE) for start in range(0, size, TILE)]

    def take(start, size):
        return pl.ds(pl.multiple_of(start, size), size)

    used = [0]
    started = []

    def send(src, dst, peer):
        k = used[0]
        used[0] += 1
        copy = pltpu.make_async_remote_copy(
            src_ref=src, dst_ref=dst, send_sem=send_sem.at[k], recv_sem=recv_sem.at[k],
            device_id=peer, device_id_type=MESH,
        )
        copy.start()
        started.append(copy)
        return copy

    loads = [
        pltpu.make_async_copy(w_in_hbm, w_in, local_sem.at[0]),
        pltpu.make_async_copy(w_out_hbm, w_out, local_sem.at[1]),
        pltpu.make_async_copy(embed_hbm, embed.at[pl.ds(0, local_vocab)], local_sem.at[2]),
    ]
    for load in loads:
        load.start()

    barrier = pltpu.get_barrier_semaphore()
    greet = [x_peer(d) for d in STEPS] + [z_peer(k) for k in Z_STEPS] + [z_source(SIDE)]
    greet += [vocab_peer(*s) for s in PEER_STEPS]
    for peer in greet:
        pl.semaphore_signal(barrier, inc=1, device_id=peer, device_id_type=MESH)

    inputs = x_ref[...].astype(F32)
    scale_in = norm_scale(inputs)
    normed = (inputs * scale_in * gain_in_ref[...]).astype(BF16)
    for c in chunks:
        fwd_all[c, 0:part, :] = normed[c * part : (c + 1) * part]
    embed[local_vocab:, :] = jnp.zeros((padded_vocab - local_vocab, D), BF16)
    pl.semaphore_wait(barrier, len(greet))

    my_slot = core * 8 + chip_slot(0, 0)

    def unit_gather(buf):
        def block(dx, k, columns=EVERY):
            return buf.at[pl.ds((dx * 4 + k) * part, part), columns]

        along_z = [send(block(0, 0), block(0, k), z_peer(k)) for k in Z_STEPS]
        along_x = [send(block(0, 0), block(4 - d, 0), x_peer(d)) for d in STEPS]
        across = along_x[:1]
        landed = along_x[1:]
        for k, copy in reversed(list(zip(Z_STEPS, along_z))):
            if k != SIDE:
                yield
            copy.wait_recv()
            for d in STEPS:
                columns = DIRECT if d == 2 else EVERY
                landed.append(send(block(0, k, columns), block(4 - d, k, columns), x_peer(d)))
            if k == NEAR:
                across[0].wait_recv()
                landed += [
                    send(block(2, 0, TURNED), block(2, m, TURNED), z_peer(m)) for m in Z_STEPS
                ]
        yield
        for copy in landed:
            copy.wait_recv()

    def unit_sum(partial, own, landing, mid, landing_z, turn, turn_mid, turn_in):
        def block(dx, k, columns=EVERY):
            return partial.at[pl.ds((dx * 4 + k) * part, part), columns]

        def rows_of(k):
            return slice(k * part, (k + 1) * part)

        turning = [send(block(2, k, TURNED), turn.at[k - 1], z_source(k)) for k in Z_STEPS]
        along_x = {}
        for k in Z_STEPS + (0,):
            along_x[k] = []
            for d in STEPS:
                columns = DIRECT if d == 2 else EVERY
                to = landing.at[d - 1, pl.ds(k * part, part), columns]
                along_x[k].append(send(block(d, k, columns), to, x_peer(d)))
        along_z = []
        for k in Z_STEPS + (0,):
            if k != NEAR:
                yield
            if k == SIDE:
                for copy in turning:
                    copy.wait_recv()
                total = partial[8 * part : 9 * part, SPLIT:].astype(F32)
                for m in range(3):
                    total = total + turn[m].astype(F32)
                turn_mid[...] = total.astype(BF16)
                turned = send(turn_mid, turn_in, x_peer(2))
            for copy in along_x[k]:
                copy.wait_recv()
            at = rows_of(k)
            total = own[at, :] + landing[0, at, :].astype(F32) + landing[2, at, :].astype(F32)
            direct = total[:, :SPLIT] + landing[1, at, :SPLIT].astype(F32)
            if k:
                mid[at, :SPLIT] = direct.astype(BF16)
                mid[at, SPLIT:] = total[:, SPLIT:].astype(BF16)
                along_z.append(send(mid.at[pl.ds(k * part, part)], landing_z.at[k - 1], z_source(k)))
        yield
        for copy in along_z + [turned]:
            copy.wait_recv()
        total = jnp.concatenate([direct, total[:, SPLIT:] + turn_in[...].astype(F32)], axis=1)
        for m in range(3):
            total = total + landing_z[m].astype(F32)
        return total

    lane = lax.broadcasted_iota(jnp.int32, (1, TILE), 1)
    half = rows // 2

    def chain(c):
        here = slice(c * part, (c + 1) * part)
        gather = unit_gather(fwd_all.at[c])
        next(gather)
        yield

        pick = eye(part, block, c * part)
        for slot in range(16):
            owner = ((slot // 4) % 2) * 8 + (slot % 4) * 2 + slot // 8
            at = slice(slot * part, (slot + 1) * part)
            label[c, at, :] = as_column(targets_ref[owner].astype(F32), pick)
            weight[c, at, :] = as_column(mask_ref[owner].astype(F32), pick)
        yield from gather

        if c == 0:
            loads[0].wait()
        for at in tiles(hidden):
            before = jnp.dot(fwd_all[c], w_in[:, at], preferred_element_type=F32)
            active[c, :, at] = jnp.maximum(before, 0.0).astype(BF16)
        if c == 0:
            loads[1].wait()
        for at in tiles(D):
            product = jnp.dot(active[c], w_out[:, at], preferred_element_type=F32)
            fwd_own[c, :, at] = product[0 : 4 * part]
            fwd_part[c, :, at] = product.astype(BF16)
        branch = yield from unit_sum(
            fwd_part.at[c], fwd_own.at[c], fwd_x.at[c], fwd_mid.at[c], fwd_z.at[c],
            fwd_turn.at[c], fwd_turn_mid.at[c], fwd_turn_in.at[c]
        )

        summed = inputs[here] + branch
        scale_out = norm_scale(summed)
        summed_ref[c] = summed
        mine = head_all.at[c, take(my_slot * part, part)]
        mine[...] = (summed * scale_out * gain_out_ref[...]).astype(BF16)
        arrivals = [send(mine, mine, vocab_peer(*s, 0)) for s in CHIP_STEPS]
        across = [send(mine, mine, vocab_peer(0, 0, 1))]
        yield
        for copy, (dzlo, dy) in reversed(list(zip(arrivals, CHIP_STEPS))):
            copy.wait_recv()
            slot = head_all.at[c, take((core * 8 + chip_slot(-dzlo, -dy)) * part, part)]
            across.append(send(slot, slot, vocab_peer(0, 0, 1)))
        yield
        for copy in across:
            copy.wait_recv()

        if c == 0:
            loads[2].wait()
        best = jnp.full((rows, 128), -1e30, F32)
        for at in tiles(padded_vocab):
            tile = lax.dot_general(head_all[c], embed[at, :], NT, preferred_element_type=F32)
            column = lane + at.start
            live = jnp.logical_and(column < local_vocab, column + vocab * local_vocab < VOCAB)
            tile = jnp.where(live, tile * factor, -1e30)
            logits[c, :, at] = tile
            for k in range(TILE // 128):
                best = jnp.maximum(best, tile[:, k * 128 : (k + 1) * 128])
        local_top = jnp.max(best, axis=1, keepdims=True)
        acc = jnp.zeros((rows, 128), F32)
        for at in tiles(padded_vocab):
            tile = jnp.exp(logits[c, :, at] - local_top)
            logits[c, :, at] = tile
            for k in range(TILE // 128):
                acc = acc + tile[:, k * 128 : (k + 1) * 128]
        local_sum = jnp.sum(acc, axis=1, keepdims=True)
        stats[c] = jnp.zeros((8, 128), F32)
        for h in range(rows // 128):
            stats[c, h : h + 1, :] = as_row(local_top[h * 128 : (h + 1) * 128])
            stats[c, 4 + h : 5 + h, :] = as_row(local_sum[h * 128 : (h + 1) * 128])
        exchange = [
            send(stats.at[c], stats_in.at[c, k], vocab_peer(*s)) for k, s in enumerate(PEER_STEPS)
        ]
        yield
        for copy in exchange:
            copy.wait_recv()

        own_top, own_sum = stats[c, 0:4, :], stats[c, 4:8, :]
        row_top = own_top
        for k in range(len(PEER_STEPS)):
            row_top = jnp.maximum(row_top, stats_in[c, k, 0:4, :])
        row_sum = own_sum * jnp.exp(own_top - row_top)
        for k in range(len(PEER_STEPS)):
            row_sum = row_sum + stats_in[c, k, 4:8, :] * jnp.exp(stats_in[c, k, 0:4, :] - row_top)
        ratio_rows = jnp.exp(own_top - row_top) / row_sum
        ratio = jnp.concatenate(
            [as_column(ratio_rows[h : h + 1], eye(128, 128)) for h in range(rows // 128)], axis=0
        )
        wanted = label[c].astype(jnp.int32) - vocab * local_vocab
        for at in tiles(padded_vocab):
            onehot = (lane + at.start == wanted).astype(F32)
            grads[c, :, at] = (weight[c] * (logits[c, :, at] * ratio - onehot)).astype(BF16)
        across = []
        for at in tiles(D):
            product = jnp.dot(grads[c], embed[:, at], preferred_element_type=F32) * factor
            head_part[c, :, at] = product.astype(BF16)
            if at.stop % 512 == 0:
                columns = pl.ds(at.stop - 512, 512)
                across.append(
                    send(
                        head_part.at[c, take((1 - core) * half, half), columns],
                        head_core.at[c, :, columns], vocab_peer(0, 0, 1),
                    )
                )
        yield
        for copy in across:
            copy.wait_recv()

        total = head_part[c, take(core * half, half), :].astype(F32) + head_core[c].astype(F32)
        head_mid[c] = total.astype(BF16)
        arrivals = [
            send(
                head_mid.at[c, take(chip_slot(*s) * part, part)], head_in.at[c, k],
                vocab_peer(*s, 0),
            )
            for k, s in enumerate(CHIP_STEPS)
        ]
        yield
        for copy in arrivals:
            copy.wait_recv()

        grad_final = head_mid[c, take(chip_slot(0, 0) * part, part), :].astype(F32)
        for k in range(len(CHIP_STEPS)):
            grad_final = grad_final + head_in[c, k].astype(F32)
        summed = summed_ref[c]
        grad_sum = norm_back(grad_final, summed, norm_scale(summed), gain_out_ref[...])
        grad_sum_ref[c] = grad_sum
        bwd_all[c, 0:part, :] = grad_sum.astype(BF16)
        yield from unit_gather(bwd_all.at[c])

        for at in tiles(hidden):
            product = lax.dot_general(bwd_all[c], w_out[at, :], NT, preferred_element_type=F32)
            held = active[c, :, at].astype(F32)
            near[c, :, at] = jnp.where(held > 0.0, product, 0.0).astype(BF16)
        for at in tiles(D):
            product = lax.dot_general(near[c], w_in[at, :], NT, preferred_element_type=F32)
            bwd_own[c, :, at] = product[0 : 4 * part]
            bwd_part[c, :, at] = product.astype(BF16)
        grad_normed = yield from unit_sum(
            bwd_part.at[c], bwd_own.at[c], bwd_x.at[c], bwd_mid.at[c], bwd_z.at[c],
            bwd_turn.at[c], bwd_turn_mid.at[c], bwd_turn_in.at[c]
        )
        out_ref[here, :] = grad_sum_ref[c] + norm_back(
            grad_normed, inputs[here], scale_in[here], gain_in_ref[...]
        )

    chains = [chain(c) for c in chunks]
    for c in ORDER:
        next(chains[c], None)
    assert len(started) == SENDS
    for copy in started:
        copy.wait_send()


def local(x_rows, gain_in, w_in, w_out, gain_out, embed, targets, row_mask):
    block = x_rows.shape[2]
    part = block // CHUNKS
    rows = 16 * part
    hidden = w_in.shape[1]
    padded_vocab = (embed.shape[0] + 511) // 512 * 512
    c = CHUNKS
    unit_sum = [
        pltpu.VMEM((c, rows, D), BF16),
        pltpu.VMEM((c, rows, D), BF16),
        pltpu.VMEM((c, 4 * part, D), F32),
        pltpu.VMEM((c, 3, 4 * part, D), BF16),
        pltpu.VMEM((c, 4 * part, D), BF16),
        pltpu.VMEM((c, 3, part, D), BF16),
        pltpu.VMEM((c, 3, part, D - SPLIT), BF16),
        pltpu.VMEM((c, part, D - SPLIT), BF16),
        pltpu.VMEM((c, part, D - SPLIT), BF16),
    ]
    scratch = [
        pltpu.VMEM(w_in.shape, BF16),
        pltpu.VMEM(w_out.shape, BF16),
        pltpu.VMEM((padded_vocab, D), BF16),
        pltpu.VMEM((c, rows, hidden), BF16),
        pltpu.VMEM((c, rows, hidden), BF16),
        pltpu.VMEM((c, rows, padded_vocab), F32),
        pltpu.VMEM((c, rows, padded_vocab), BF16),
        pltpu.VMEM((c, rows, 1), F32),
        pltpu.VMEM((c, rows, 1), F32),
        *unit_sum,
        pltpu.VMEM((c, rows, D), BF16),
        pltpu.VMEM((c, 8, 128), F32),
        pltpu.VMEM((c, 15, 8, 128), F32),
        pltpu.VMEM((c, rows, D), BF16),
        pltpu.VMEM((c, rows // 2, D), BF16),
        pltpu.VMEM((c, rows // 2, D), BF16),
        pltpu.VMEM((c, 7, part, D), BF16),
        *unit_sum,
        pltpu.VMEM((c, part, D), F32),
        pltpu.VMEM((c, part, D), F32),
        pltpu.SemaphoreType.DMA((3,)),
        pltpu.SemaphoreType.DMA((SENDS,)),
        pltpu.SemaphoreType.DMA((SENDS,)),
    ]
    vmem = pl.BlockSpec(memory_space=pltpu.VMEM)
    anywhere = pl.BlockSpec(memory_space=pl.ANY)
    result = pl.pallas_call(
        kernel,
        out_shape=jax.ShapeDtypeStruct((block, D), F32),
        in_specs=[vmem, vmem, anywhere, anywhere, vmem, anywhere, vmem, vmem],
        out_specs=vmem,
        scratch_shapes=scratch,
        compiler_params=pltpu.CompilerParams(
            collective_id=0, has_side_effects=True, vmem_limit_bytes=56 * 1024 * 1024
        ),
        cost_estimate=pl.CostEstimate(
            flops=12 * 512 * D * hidden, bytes_accessed=6 * hidden * D, transcendentals=0
        ),
    )(
        x_rows.reshape(block, D), gain_in.reshape(1, D), w_in, w_out, gain_out.reshape(1, D), embed,
        targets, row_mask,
    )
    return result.reshape(1, 1, block, D)


def solution(mesh):
    in_specs = (
        P("vocab", "units", None, None),
        P(),
        P(None, "units"),
        P("units", None),
        P(),
        P("vocab", None),
        P(None, "units", None),
        P(None, "units", None),
    )
    out_specs = P("vocab", "units", None, None)
    return jax.shard_map(local, mesh=mesh, in_specs=in_specs, out_specs=out_specs, check_vma=False)
```

```python
import functools
import math

import jax
import jax.numpy as jnp
from jax import lax
from jax.experimental import pallas as pl
from jax.experimental.pallas import tpu as pltpu
from jax.sharding import PartitionSpec as P

D = 1024
VOCAB = 32128
EPSILON = 1e-06
CHUNKS = 2
TILE = 256
SENDS = 113 * CHUNKS
ORDER = [int(c) for c in "0100110100011101010101010100110100011101"]
F32, BF16 = jnp.float32, jnp.bfloat16
MESH = pl.DeviceIdType.MESH
STEPS = (2, 1, 3)
NEAR, SIDE, FAR = 1, 2, 3
Z_STEPS = (FAR, SIDE, NEAR)
SPLIT = 256
EVERY, DIRECT, TURNED = pl.ds(0, D), pl.ds(0, SPLIT), pl.ds(SPLIT, D - SPLIT)
CHIP_STEPS = ((1, 2), (0, 2), (1, 1), (1, 3), (0, 1), (0, 3), (1, 0))
PEER_STEPS = tuple(s + (c,) for s in CHIP_STEPS for c in (0, 1)) + ((0, 0, 1),)
NT = (((1,), (1,)), ((), ()))


def norm_scale(values):
    return lax.rsqrt(jnp.mean(values * values, axis=-1, keepdims=True) + EPSILON)


def norm_back(grad_in, values, scale_rows, gain_vec):
    scaled = grad_in * gain_vec
    inner_sum = jnp.mean(scaled * values, axis=-1, keepdims=True)
    return scaled * scale_rows - values * (scale_rows * scale_rows * scale_rows) * inner_sum


def eye(rows, columns, shift=0):
    row = lax.broadcasted_iota(jnp.int32, (rows, columns), 0)
    return row + shift == lax.broadcasted_iota(jnp.int32, (rows, columns), 1)


def as_row(column):
    return jnp.sum(jnp.where(eye(128, 128), column, 0.0), axis=0, keepdims=True)


def as_column(row, mask):
    return jnp.sum(jnp.where(mask, row, 0.0), axis=1, keepdims=True)


def kernel(
    x_hbm, gain_in_hbm, w_in_hbm, w_out_hbm, gain_out_hbm, embed_hbm, targets_hbm, mask_hbm,
    out_ref,
    x_ref, gain_in_ref, gain_out_ref, targets_ref, mask_ref,
    w_in, w_out, embed, near, active, logits, grads, label, weight,
    fwd_all, fwd_part, fwd_own, fwd_x, fwd_mid, fwd_z, fwd_turn, fwd_turn_mid, fwd_turn_in,
    head_all, stats, stats_in, head_part, head_core, head_mid, head_in,
    bwd_all, bwd_part, bwd_own, bwd_x, bwd_mid, bwd_z, bwd_turn, bwd_turn_mid, bwd_turn_in,
    summed_ref, grad_sum_ref, local_sem, send_sem, recv_sem,
):
    vocab = lax.axis_index("vocab")
    unit = lax.axis_index("units")
    x_at, z_at = unit // 4, unit % 4
    core, y_at, zlo_at = vocab % 2, (vocab // 2) % 4, vocab // 8
    local_vocab = embed_hbm.shape[0]
    padded_vocab = embed.shape[0]
    block = x_ref.shape[0]
    part = block // CHUNKS
    rows = 16 * part
    hidden = w_in.shape[1]
    factor = 1.0 / math.sqrt(D)
    chunks = range(CHUNKS)

    def x_peer(dx):
        return vocab, ((x_at + dx) % 4) * 4 + z_at

    towards = 2 * zlo_at - 1

    def z_chip(z_hi, z_lo):
        return z_lo * 8 + y_at * 2 + core, x_at * 4 + z_hi % 4

    def z_peer(k):
        if k == SIDE:
            return z_chip(z_at + 4 - towards, zlo_at)
        return z_chip(z_at + (4 + towards if k == NEAR else 2), 1 - zlo_at)

    def z_source(k):
        return z_chip(z_at + 4 + towards, zlo_at) if k == SIDE else z_peer(k)

    def vocab_peer(dzlo, dy, dcore):
        return ((zlo_at + dzlo) % 2) * 8 + ((y_at + dy) % 4) * 2 + (core + dcore) % 2, unit

    def chip_slot(dzlo, dy):
        return ((zlo_at + dzlo) % 2) * 4 + (y_at + dy) % 4

    def tiles(size):
        return [slice(start, start + TILE) for start in range(0, size, TILE)]

    def take(start, size):
        return pl.ds(pl.multiple_of(start, size), size)

    used = [0]
    started = []

    def send(src, dst, peer):
        k = used[0]
        used[0] += 1
        copy = pltpu.make_async_remote_copy(
            src_ref=src, dst_ref=dst, send_sem=send_sem.at[k], recv_sem=recv_sem.at[k],
            device_id=peer, device_id_type=MESH,
        )
        copy.start()
        started.append(copy)
        return copy

    barrier = pltpu.get_barrier_semaphore()
    greet = [x_peer(d) for d in STEPS] + [z_peer(k) for k in Z_STEPS] + [z_source(SIDE)]
    greet += [vocab_peer(*s) for s in PEER_STEPS]
    for peer in greet:
        pl.semaphore_signal(barrier, inc=1, device_id=peer, device_id_type=MESH)

    small = [
        pltpu.make_async_copy(src, dst, local_sem.at[3 + k])
        for k, (src, dst) in enumerate(
            (
                (x_hbm, x_ref), (gain_in_hbm, gain_in_ref), (gain_out_hbm, gain_out_ref),
                (targets_hbm, targets_ref), (mask_hbm, mask_ref),
            )
        )
    ]
    loads = [
        pltpu.make_async_copy(w_in_hbm, w_in, local_sem.at[0]),
        pltpu.make_async_copy(w_out_hbm, w_out, local_sem.at[1]),
        pltpu.make_async_copy(embed_hbm, embed.at[pl.ds(0, local_vocab)], local_sem.at[2]),
    ]
    for load in small + loads:
        load.start()
    embed[local_vocab:, :] = jnp.zeros((padded_vocab - local_vocab, D), BF16)
    for load in small:
        load.wait()

    inputs = x_ref[...].astype(F32)
    scale_in = norm_scale(inputs)
    normed = (inputs * scale_in * gain_in_ref[...]).astype(BF16)
    for c in chunks:
        fwd_all[c, 0:part, :] = normed[c * part : (c + 1) * part]
    pl.semaphore_wait(barrier, len(greet))

    my_slot = core * 8 + chip_slot(0, 0)

    def unit_gather(buf):
        def block(dx, k, columns=EVERY):
            return buf.at[pl.ds((dx * 4 + k) * part, part), columns]

        along_z = [send(block(0, 0), block(0, k), z_peer(k)) for k in Z_STEPS]
        along_x = [send(block(0, 0), block(4 - d, 0), x_peer(d)) for d in STEPS]
        across = along_x[:1]
        landed = along_x[1:]
        for k, copy in reversed(list(zip(Z_STEPS, along_z))):
            if k != SIDE:
                yield
            copy.wait_recv()
            for d in STEPS:
                columns = DIRECT if d == 2 else EVERY
                landed.append(send(block(0, k, columns), block(4 - d, k, columns), x_peer(d)))
            if k == FAR:
                across[0].wait_recv()
                landed += [
                    send(block(2, 0, TURNED), block(2, m, TURNED), z_peer(m)) for m in Z_STEPS
                ]
        yield
        for copy in landed:
            copy.wait_recv()

    def unit_sum(partial, own, landing, mid, landing_z, turn, turn_mid, turn_in):
        def block(dx, k, columns=EVERY):
            return partial.at[pl.ds((dx * 4 + k) * part, part), columns]

        def rows_of(k):
            return slice(k * part, (k + 1) * part)

        turning = [send(block(2, k, TURNED), turn.at[k - 1], z_source(k)) for k in Z_STEPS]
        along_x = {}
        for k in Z_STEPS + (0,):
            along_x[k] = []
            for d in STEPS:
                columns = DIRECT if d == 2 else EVERY
                to = landing.at[d - 1, pl.ds(k * part, part), columns]
                along_x[k].append(send(block(d, k, columns), to, x_peer(d)))
        along_z = []
        for k in Z_STEPS + (0,):
            if k != NEAR:
                yield
            if k == SIDE:
                for copy in turning:
                    copy.wait_recv()
                total = partial[8 * part : 9 * part, SPLIT:].astype(F32)
                for m in range(3):
                    total = total + turn[m].astype(F32)
                turn_mid[...] = total.astype(BF16)
                turned = send(turn_mid, turn_in, x_peer(2))
            for copy in along_x[k]:
                copy.wait_recv()
            at = rows_of(k)
            total = own[at, :] + landing[0, at, :].astype(F32) + landing[2, at, :].astype(F32)
            direct = total[:, :SPLIT] + landing[1, at, :SPLIT].astype(F32)
            if k:
                mid[at, :SPLIT] = direct.astype(BF16)
                mid[at, SPLIT:] = total[:, SPLIT:].astype(BF16)
                along_z.append(send(mid.at[pl.ds(k * part, part)], landing_z.at[k - 1], z_source(k)))
        yield
        for copy in along_z + [turned]:
            copy.wait_recv()
        total = jnp.concatenate([direct, total[:, SPLIT:] + turn_in[...].astype(F32)], axis=1)
        for m in range(3):
            total = total + landing_z[m].astype(F32)
        return total

    lane = lax.broadcasted_iota(jnp.int32, (1, TILE), 1)
    half = rows // 2

    def chain(c):
        here = slice(c * part, (c + 1) * part)
        gather = unit_gather(fwd_all.at[c])
        next(gather)
        yield

        pick = eye(part, block, c * part)
        for slot in range(16):
            owner = ((slot // 4) % 2) * 8 + (slot % 4) * 2 + slot // 8
            at = slice(slot * part, (slot + 1) * part)
            label[c, at, :] = as_column(targets_ref[owner].astype(F32), pick)
            weight[c, at, :] = as_column(mask_ref[owner].astype(F32), pick)
        yield from gather

        if c == 0:
            loads[0].wait()
        for at in tiles(hidden):
            before = jnp.dot(fwd_all[c], w_in[:, at], preferred_element_type=F32)
            active[c, :, at] = jnp.maximum(before, 0.0).astype(BF16)
        if c == 0:
            loads[1].wait()
        for at in tiles(D):
            product = jnp.dot(active[c], w_out[:, at], preferred_element_type=F32)
            fwd_own[c, :, at] = product[0 : 4 * part]
            fwd_part[c, :, at] = product.astype(BF16)
        branch = yield from unit_sum(
            fwd_part.at[c], fwd_own.at[c], fwd_x.at[c], fwd_mid.at[c], fwd_z.at[c],
            fwd_turn.at[c], fwd_turn_mid.at[c], fwd_turn_in.at[c]
        )

        summed = inputs[here] + branch
        scale_out = norm_scale(summed)
        summed_ref[c] = summed
        mine = head_all.at[c, take(my_slot * part, part)]
        mine[...] = (summed * scale_out * gain_out_ref[...]).astype(BF16)
        arrivals = [send(mine, mine, vocab_peer(*s, 0)) for s in CHIP_STEPS]
        across = [send(mine, mine, vocab_peer(0, 0, 1))]
        yield
        for copy, (dzlo, dy) in reversed(list(zip(arrivals, CHIP_STEPS))):
            copy.wait_recv()
            slot = head_all.at[c, take((core * 8 + chip_slot(-dzlo, -dy)) * part, part)]
            across.append(send(slot, slot, vocab_peer(0, 0, 1)))
        yield
        for copy in across:
            copy.wait_recv()

        if c == 0:
            loads[2].wait()
        best = jnp.full((rows, 128), -1e30, F32)
        for at in tiles(padded_vocab):
            tile = lax.dot_general(head_all[c], embed[at, :], NT, preferred_element_type=F32)
            column = lane + at.start
            live = jnp.logical_and(column < local_vocab, column + vocab * local_vocab < VOCAB)
            tile = jnp.where(live, tile * factor, -1e30)
            logits[c, :, at] = tile
            for k in range(TILE // 128):
                best = jnp.maximum(best, tile[:, k * 128 : (k + 1) * 128])
        local_top = jnp.max(best, axis=1, keepdims=True)
        acc = jnp.zeros((rows, 128), F32)
        for at in tiles(padded_vocab):
            tile = jnp.exp(logits[c, :, at] - local_top)
            logits[c, :, at] = tile
            for k in range(TILE // 128):
                acc = acc + tile[:, k * 128 : (k + 1) * 128]
        local_sum = jnp.sum(acc, axis=1, keepdims=True)
        stats[c] = jnp.zeros((8, 128), F32)
        for h in range(rows // 128):
            stats[c, h : h + 1, :] = as_row(local_top[h * 128 : (h + 1) * 128])
            stats[c, 4 + h : 5 + h, :] = as_row(local_sum[h * 128 : (h + 1) * 128])
        exchange = [
            send(stats.at[c], stats_in.at[c, k], vocab_peer(*s)) for k, s in enumerate(PEER_STEPS)
        ]
        yield
        for copy in exchange:
            copy.wait_recv()

        own_top, own_sum = stats[c, 0:4, :], stats[c, 4:8, :]
        row_top = own_top
        for k in range(len(PEER_STEPS)):
            row_top = jnp.maximum(row_top, stats_in[c, k, 0:4, :])
        row_sum = own_sum * jnp.exp(own_top - row_top)
        for k in range(len(PEER_STEPS)):
            row_sum = row_sum + stats_in[c, k, 4:8, :] * jnp.exp(stats_in[c, k, 0:4, :] - row_top)
        ratio_rows = jnp.exp(own_top - row_top) / row_sum
        ratio = jnp.concatenate(
            [as_column(ratio_rows[h : h + 1], eye(128, 128)) for h in range(rows // 128)], axis=0
        )
        wanted = label[c].astype(jnp.int32) - vocab * local_vocab
        for at in tiles(padded_vocab):
            onehot = (lane + at.start == wanted).astype(F32)
            grads[c, :, at] = (weight[c] * (logits[c, :, at] * ratio - onehot)).astype(BF16)
        across = []
        for at in tiles(D):
            product = jnp.dot(grads[c], embed[:, at], preferred_element_type=F32) * factor
            head_part[c, :, at] = product.astype(BF16)
            if at.stop % 512 == 0:
                columns = pl.ds(at.stop - 512, 512)
                across.append(
                    send(
                        head_part.at[c, take((1 - core) * half, half), columns],
                        head_core.at[c, :, columns], vocab_peer(0, 0, 1),
                    )
                )
        yield
        for copy in across:
            copy.wait_recv()

        total = head_part[c, take(core * half, half), :].astype(F32) + head_core[c].astype(F32)
        head_mid[c] = total.astype(BF16)
        arrivals = [
            send(
                head_mid.at[c, take(chip_slot(*s) * part, part)], head_in.at[c, k],
                vocab_peer(*s, 0),
            )
            for k, s in enumerate(CHIP_STEPS)
        ]
        yield
        for copy in arrivals:
            copy.wait_recv()

        grad_final = head_mid[c, take(chip_slot(0, 0) * part, part), :].astype(F32)
        for k in range(len(CHIP_STEPS)):
            grad_final = grad_final + head_in[c, k].astype(F32)
        summed = summed_ref[c]
        grad_sum = norm_back(grad_final, summed, norm_scale(summed), gain_out_ref[...])
        grad_sum_ref[c] = grad_sum
        bwd_all[c, 0:part, :] = grad_sum.astype(BF16)
        yield from unit_gather(bwd_all.at[c])

        for at in tiles(hidden):
            product = lax.dot_general(bwd_all[c], w_out[at, :], NT, preferred_element_type=F32)
            held = active[c, :, at].astype(F32)
            near[c, :, at] = jnp.where(held > 0.0, product, 0.0).astype(BF16)
        for at in tiles(D):
            product = lax.dot_general(near[c], w_in[at, :], NT, preferred_element_type=F32)
            bwd_own[c, :, at] = product[0 : 4 * part]
            bwd_part[c, :, at] = product.astype(BF16)
        grad_normed = yield from unit_sum(
            bwd_part.at[c], bwd_own.at[c], bwd_x.at[c], bwd_mid.at[c], bwd_z.at[c],
            bwd_turn.at[c], bwd_turn_mid.at[c], bwd_turn_in.at[c]
        )
        out_ref[here, :] = grad_sum_ref[c] + norm_back(
            grad_normed, inputs[here], scale_in[here], gain_in_ref[...]
        )

    chains = [chain(c) for c in chunks]
    for c in ORDER:
        next(chains[c], None)
    assert len(started) == SENDS
    for copy in started:
        copy.wait_send()


def local(x_rows, gain_in, w_in, w_out, gain_out, embed, targets, row_mask):
    block = x_rows.shape[2]
    part = block // CHUNKS
    rows = 16 * part
    hidden = w_in.shape[1]
    padded_vocab = (embed.shape[0] + 511) // 512 * 512
    c = CHUNKS
    unit_sum = [
        pltpu.VMEM((c, rows, D), BF16),
        pltpu.VMEM((c, rows, D), BF16),
        pltpu.VMEM((c, 4 * part, D), F32),
        pltpu.VMEM((c, 3, 4 * part, D), BF16),
        pltpu.VMEM((c, 4 * part, D), BF16),
        pltpu.VMEM((c, 3, part, D), BF16),
        pltpu.VMEM((c, 3, part, D - SPLIT), BF16),
        pltpu.VMEM((c, part, D - SPLIT), BF16),
        pltpu.VMEM((c, part, D - SPLIT), BF16),
    ]
    scratch = [
        pltpu.VMEM((block, D), BF16),
        pltpu.VMEM((1, D), F32),
        pltpu.VMEM((1, D), F32),
        pltpu.VMEM(targets.shape, jnp.int32),
        pltpu.VMEM(row_mask.shape, jnp.int32),
        pltpu.VMEM(w_in.shape, BF16),
        pltpu.VMEM(w_out.shape, BF16),
        pltpu.VMEM((padded_vocab, D), BF16),
        pltpu.VMEM((c, rows, hidden), BF16),
        pltpu.VMEM((c, rows, hidden), BF16),
        pltpu.VMEM((c, rows, padded_vocab), F32),
        pltpu.VMEM((c, rows, padded_vocab), BF16),
        pltpu.VMEM((c, rows, 1), F32),
        pltpu.VMEM((c, rows, 1), F32),
        *unit_sum,
        pltpu.VMEM((c, rows, D), BF16),
        pltpu.VMEM((c, 8, 128), F32),
        pltpu.VMEM((c, 15, 8, 128), F32),
        pltpu.VMEM((c, rows, D), BF16),
        pltpu.VMEM((c, rows // 2, D), BF16),
        pltpu.VMEM((c, rows // 2, D), BF16),
        pltpu.VMEM((c, 7, part, D), BF16),
        *unit_sum,
        pltpu.VMEM((c, part, D), F32),
        pltpu.VMEM((c, part, D), F32),
        pltpu.SemaphoreType.DMA((8,)),
        pltpu.SemaphoreType.DMA((SENDS,)),
        pltpu.SemaphoreType.DMA((SENDS,)),
    ]
    vmem = pl.BlockSpec(memory_space=pltpu.VMEM)
    anywhere = pl.BlockSpec(memory_space=pl.ANY)
    result = pl.pallas_call(
        kernel,
        out_shape=jax.ShapeDtypeStruct((block, D), F32),
        in_specs=[anywhere] * 8,
        out_specs=vmem,
        scratch_shapes=scratch,
        compiler_params=pltpu.CompilerParams(
            collective_id=0, has_side_effects=True, vmem_limit_bytes=56 * 1024 * 1024
        ),
        cost_estimate=pl.CostEstimate(
            flops=12 * 512 * D * hidden, bytes_accessed=6 * hidden * D, transcendentals=0
        ),
    )(
        x_rows.reshape(block, D), gain_in.reshape(1, D), w_in, w_out, gain_out.reshape(1, D), embed,
        targets, row_mask,
    )
    return result.reshape(1, 1, block, D)


def solution(mesh):
    in_specs = (
        P("vocab", "units", None, None),
        P(),
        P(None, "units"),
        P("units", None),
        P(),
        P("vocab", None),
        P(None, "units", None),
        P(None, "units", None),
    )
    out_specs = P("vocab", "units", None, None)
    return jax.shard_map(local, mesh=mesh, in_specs=in_specs, out_specs=out_specs, check_vma=False)
```

```python
import functools
import math

import jax
import jax.numpy as jnp
from jax import lax
from jax.experimental import pallas as pl
from jax.experimental.pallas import tpu as pltpu
from jax.sharding import PartitionSpec as P

D = 1024
VOCAB = 32128
EPSILON = 1e-06
CHUNKS = 2
TILE = 256
SENDS = 113 * CHUNKS
ORDER = [int(c) for c in "0100110100011101010101010100110100011101"]
F32, BF16 = jnp.float32, jnp.bfloat16
MESH = pl.DeviceIdType.MESH
STEPS = (2, 1, 3)
NEAR, SIDE, FAR = 1, 2, 3
Z_STEPS = (FAR, SIDE, NEAR)
SPLIT = 256
EVERY, DIRECT, TURNED = pl.ds(0, D), pl.ds(0, SPLIT), pl.ds(SPLIT, D - SPLIT)
CHIP_STEPS = ((1, 2), (0, 2), (1, 1), (1, 3), (0, 1), (0, 3), (1, 0))
PEER_STEPS = tuple(s + (c,) for s in CHIP_STEPS for c in (0, 1)) + ((0, 0, 1),)
NT = (((1,), (1,)), ((), ()))


def norm_scale(values):
    return lax.rsqrt(jnp.mean(values * values, axis=-1, keepdims=True) + EPSILON)


def norm_back(grad_in, values, scale_rows, gain_vec):
    scaled = grad_in * gain_vec
    inner_sum = jnp.mean(scaled * values, axis=-1, keepdims=True)
    return scaled * scale_rows - values * (scale_rows * scale_rows * scale_rows) * inner_sum


def eye(rows, columns, shift=0):
    row = lax.broadcasted_iota(jnp.int32, (rows, columns), 0)
    return row + shift == lax.broadcasted_iota(jnp.int32, (rows, columns), 1)


def as_row(column):
    return jnp.sum(jnp.where(eye(128, 128), column, 0.0), axis=0, keepdims=True)


def as_column(row, mask):
    return jnp.sum(jnp.where(mask, row, 0.0), axis=1, keepdims=True)


def kernel(
    x_hbm, gain_in_hbm, w_in_hbm, w_out_hbm, gain_out_hbm, embed_hbm, targets_hbm, mask_hbm,
    out_ref,
    x_ref, gain_in_ref, gain_out_ref, targets_ref, mask_ref,
    w_in, w_out, embed, near, active, logits, grads, label, weight,
    fwd_all, fwd_part, fwd_own, fwd_x, fwd_mid, fwd_z, fwd_turn, fwd_turn_mid, fwd_turn_in,
    head_all, stats, stats_in, head_part, head_core, head_mid, head_in,
    bwd_all, bwd_part, bwd_own, bwd_x, bwd_mid, bwd_z, bwd_turn, bwd_turn_mid, bwd_turn_in,
    summed_ref, grad_sum_ref, local_sem, send_sem, recv_sem,
):
    vocab = lax.axis_index("vocab")
    unit = lax.axis_index("units")
    x_at, z_at = unit // 4, unit % 4
    core, y_at, zlo_at = vocab % 2, (vocab // 2) % 4, vocab // 8
    local_vocab = embed_hbm.shape[0]
    padded_vocab = embed.shape[0]
    block = x_ref.shape[0]
    part = block // CHUNKS
    rows = 16 * part
    hidden = w_in.shape[1]
    factor = 1.0 / math.sqrt(D)
    chunks = range(CHUNKS)

    def x_peer(dx):
        return vocab, ((x_at + dx) % 4) * 4 + z_at

    towards = 2 * zlo_at - 1

    def z_chip(z_hi, z_lo):
        return z_lo * 8 + y_at * 2 + core, x_at * 4 + z_hi % 4

    def z_peer(k):
        if k == SIDE:
            return z_chip(z_at + 4 - towards, zlo_at)
        return z_chip(z_at + (4 + towards if k == NEAR else 2), 1 - zlo_at)

    def z_source(k):
        return z_chip(z_at + 4 + towards, zlo_at) if k == SIDE else z_peer(k)

    def vocab_peer(dzlo, dy, dcore):
        return ((zlo_at + dzlo) % 2) * 8 + ((y_at + dy) % 4) * 2 + (core + dcore) % 2, unit

    def chip_slot(dzlo, dy):
        return ((zlo_at + dzlo) % 2) * 4 + (y_at + dy) % 4

    def tiles(size):
        return [slice(start, start + TILE) for start in range(0, size, TILE)]

    def take(start, size):
        return pl.ds(pl.multiple_of(start, size), size)

    used = [0]
    started = []

    def send(src, dst, peer):
        k = used[0]
        used[0] += 1
        copy = pltpu.make_async_remote_copy(
            src_ref=src, dst_ref=dst, send_sem=send_sem.at[k], recv_sem=recv_sem.at[k],
            device_id=peer, device_id_type=MESH,
        )
        copy.start()
        started.append(copy)
        return copy

    barrier = pltpu.get_barrier_semaphore()
    greet = [x_peer(d) for d in STEPS] + [z_peer(k) for k in Z_STEPS] + [z_source(SIDE)]
    greet += [vocab_peer(*s) for s in PEER_STEPS]
    for peer in greet:
        pl.semaphore_signal(barrier, inc=1, device_id=peer, device_id_type=MESH)

    small = [
        pltpu.make_async_copy(src, dst, local_sem.at[3 + k])
        for k, (src, dst) in enumerate(
            (
                (x_hbm, x_ref), (gain_in_hbm, gain_in_ref), (gain_out_hbm, gain_out_ref),
                (targets_hbm, targets_ref), (mask_hbm, mask_ref),
            )
        )
    ]
    loads = [
        pltpu.make_async_copy(w_in_hbm, w_in, local_sem.at[0]),
        pltpu.make_async_copy(w_out_hbm, w_out, local_sem.at[1]),
        pltpu.make_async_copy(embed_hbm, embed.at[pl.ds(0, local_vocab)], local_sem.at[2]),
    ]
    for load in small + loads:
        load.start()
    embed[local_vocab:, :] = jnp.zeros((padded_vocab - local_vocab, D), BF16)
    for load in small:
        load.wait()

    inputs = x_ref[...].astype(F32)
    scale_in = norm_scale(inputs)
    normed = (inputs * scale_in * gain_in_ref[...]).astype(BF16)
    for c in chunks:
        fwd_all[c, 0:part, :] = normed[c * part : (c + 1) * part]
    pl.semaphore_wait(barrier, len(greet))

    my_slot = core * 8 + chip_slot(0, 0)

    def unit_gather(buf):
        def block(dx, k, columns=EVERY):
            return buf.at[pl.ds((dx * 4 + k) * part, part), columns]

        along_z = [send(block(0, 0), block(0, k), z_peer(k)) for k in Z_STEPS]
        along_x = [send(block(0, 0), block(4 - d, 0), x_peer(d)) for d in STEPS]
        across = along_x[:1]
        landed = along_x[1:]
        for k, copy in reversed(list(zip(Z_STEPS, along_z))):
            if k != SIDE:
                yield
            copy.wait_recv()
            for d in STEPS:
                columns = DIRECT if d == 2 else EVERY
                landed.append(send(block(0, k, columns), block(4 - d, k, columns), x_peer(d)))
            if k == FAR:
                across[0].wait_recv()
                landed += [
                    send(block(2, 0, TURNED), block(2, m, TURNED), z_peer(m)) for m in Z_STEPS
                ]
        yield
        for copy in landed:
            copy.wait_recv()

    def unit_sum(partial, own, landing, mid, landing_z, turn, turn_mid, turn_in):
        def block(dx, k, columns=EVERY):
            return partial.at[pl.ds((dx * 4 + k) * part, part), columns]

        def rows_of(k):
            return slice(k * part, (k + 1) * part)

        turning = [send(block(2, k, TURNED), turn.at[k - 1], z_source(k)) for k in Z_STEPS]
        along_x = {}
        for k in Z_STEPS + (0,):
            along_x[k] = []
            for d in STEPS:
                columns = DIRECT if d == 2 else EVERY
                to = landing.at[d - 1, pl.ds(k * part, part), columns]
                along_x[k].append(send(block(d, k, columns), to, x_peer(d)))
        along_z = []
        for k in Z_STEPS + (0,):
            if k != NEAR:
                yield
            if k == SIDE:
                for copy in turning:
                    copy.wait_recv()
                total = partial[8 * part : 9 * part, SPLIT:].astype(F32)
                for m in range(3):
                    total = total + turn[m].astype(F32)
                turn_mid[...] = total.astype(BF16)
                turned = send(turn_mid, turn_in, x_peer(2))
            for copy in along_x[k]:
                copy.wait_recv()
            at = rows_of(k)
            total = own[at, :] + landing[0, at, :].astype(F32) + landing[2, at, :].astype(F32)
            direct = total[:, :SPLIT] + landing[1, at, :SPLIT].astype(F32)
            if k:
                mid[at, :SPLIT] = direct.astype(BF16)
                mid[at, SPLIT:] = total[:, SPLIT:].astype(BF16)
                along_z.append(send(mid.at[pl.ds(k * part, part)], landing_z.at[k - 1], z_source(k)))
        yield
        for copy in along_z + [turned]:
            copy.wait_recv()
        total = jnp.concatenate([direct, total[:, SPLIT:] + turn_in[...].astype(F32)], axis=1)
        for m in range(3):
            total = total + landing_z[m].astype(F32)
        return total

    lane = lax.broadcasted_iota(jnp.int32, (1, TILE), 1)
    half = rows // 2

    def chain(c):
        here = slice(c * part, (c + 1) * part)
        gather = unit_gather(fwd_all.at[c])
        next(gather)
        yield

        for k in chunks if c == 0 else ():
            pick = eye(part, block, k * part)
            for slot in range(16):
                owner = ((slot // 4) % 2) * 8 + (slot % 4) * 2 + slot // 8
                at = slice(slot * part, (slot + 1) * part)
                label[k, at, :] = as_column(targets_ref[owner].astype(F32), pick)
                weight[k, at, :] = as_column(mask_ref[owner].astype(F32), pick)
        yield from gather

        if c == 0:
            loads[0].wait()
        for at in tiles(hidden):
            before = jnp.dot(fwd_all[c], w_in[:, at], preferred_element_type=F32)
            active[c, :, at] = jnp.maximum(before, 0.0).astype(BF16)
        if c == 0:
            loads[1].wait()
        for at in tiles(D):
            product = jnp.dot(active[c], w_out[:, at], preferred_element_type=F32)
            fwd_own[c, :, at] = product[0 : 4 * part]
            fwd_part[c, :, at] = product.astype(BF16)
        branch = yield from unit_sum(
            fwd_part.at[c], fwd_own.at[c], fwd_x.at[c], fwd_mid.at[c], fwd_z.at[c],
            fwd_turn.at[c], fwd_turn_mid.at[c], fwd_turn_in.at[c]
        )

        summed = inputs[here] + branch
        scale_out = norm_scale(summed)
        summed_ref[c] = summed
        mine = head_all.at[c, take(my_slot * part, part)]
        mine[...] = (summed * scale_out * gain_out_ref[...]).astype(BF16)
        arrivals = [send(mine, mine, vocab_peer(*s, 0)) for s in CHIP_STEPS]
        across = [send(mine, mine, vocab_peer(0, 0, 1))]
        yield
        for copy, (dzlo, dy) in reversed(list(zip(arrivals, CHIP_STEPS))):
            copy.wait_recv()
            slot = head_all.at[c, take((core * 8 + chip_slot(-dzlo, -dy)) * part, part)]
            across.append(send(slot, slot, vocab_peer(0, 0, 1)))
        yield
        for copy in across:
            copy.wait_recv()

        if c == 0:
            loads[2].wait()
        best = jnp.full((rows, 128), -1e30, F32)
        for at in tiles(padded_vocab):
            tile = lax.dot_general(head_all[c], embed[at, :], NT, preferred_element_type=F32)
            column = lane + at.start
            live = jnp.logical_and(column < local_vocab, column + vocab * local_vocab < VOCAB)
            tile = jnp.where(live, tile * factor, -1e30)
            logits[c, :, at] = tile
            for k in range(TILE // 128):
                best = jnp.maximum(best, tile[:, k * 128 : (k + 1) * 128])
        local_top = jnp.max(best, axis=1, keepdims=True)
        acc = jnp.zeros((rows, 128), F32)
        for at in tiles(padded_vocab):
            tile = jnp.exp(logits[c, :, at] - local_top)
            logits[c, :, at] = tile
            for k in range(TILE // 128):
                acc = acc + tile[:, k * 128 : (k + 1) * 128]
        local_sum = jnp.sum(acc, axis=1, keepdims=True)
        stats[c] = jnp.zeros((8, 128), F32)
        for h in range(rows // 128):
            stats[c, h : h + 1, :] = as_row(local_top[h * 128 : (h + 1) * 128])
            stats[c, 4 + h : 5 + h, :] = as_row(local_sum[h * 128 : (h + 1) * 128])
        exchange = [
            send(stats.at[c], stats_in.at[c, k], vocab_peer(*s)) for k, s in enumerate(PEER_STEPS)
        ]
        yield
        wanted = label[c].astype(jnp.int32) - vocab * local_vocab
        for copy in exchange:
            copy.wait_recv()

        own_top, own_sum = stats[c, 0:4, :], stats[c, 4:8, :]
        row_top = own_top
        for k in range(len(PEER_STEPS)):
            row_top = jnp.maximum(row_top, stats_in[c, k, 0:4, :])
        row_sum = own_sum * jnp.exp(own_top - row_top)
        for k in range(len(PEER_STEPS)):
            row_sum = row_sum + stats_in[c, k, 4:8, :] * jnp.exp(stats_in[c, k, 0:4, :] - row_top)
        ratio_rows = jnp.exp(own_top - row_top) / row_sum
        ratio = jnp.concatenate(
            [as_column(ratio_rows[h : h + 1], eye(128, 128)) for h in range(rows // 128)], axis=0
        )
        for at in tiles(padded_vocab):
            onehot = (lane + at.start == wanted).astype(F32)
            grads[c, :, at] = (weight[c] * (logits[c, :, at] * ratio - onehot)).astype(BF16)
        across = []
        for at in tiles(D):
            product = jnp.dot(grads[c], embed[:, at], preferred_element_type=F32) * factor
            head_part[c, :, at] = product.astype(BF16)
            if at.stop % 512 == 0:
                columns = pl.ds(at.stop - 512, 512)
                across.append(
                    send(
                        head_part.at[c, take((1 - core) * half, half), columns],
                        head_core.at[c, :, columns], vocab_peer(0, 0, 1),
                    )
                )
        yield
        for copy in across:
            copy.wait_recv()

        total = head_part[c, take(core * half, half), :].astype(F32) + head_core[c].astype(F32)
        head_mid[c] = total.astype(BF16)
        arrivals = [
            send(
                head_mid.at[c, take(chip_slot(*s) * part, part)], head_in.at[c, k],
                vocab_peer(*s, 0),
            )
            for k, s in enumerate(CHIP_STEPS)
        ]
        yield
        summed = summed_ref[c]
        scale_out = norm_scale(summed)
        for copy in arrivals:
            copy.wait_recv()

        grad_final = head_mid[c, take(chip_slot(0, 0) * part, part), :].astype(F32)
        for k in range(len(CHIP_STEPS)):
            grad_final = grad_final + head_in[c, k].astype(F32)
        grad_sum = norm_back(grad_final, summed, scale_out, gain_out_ref[...])
        grad_sum_ref[c] = grad_sum
        bwd_all[c, 0:part, :] = grad_sum.astype(BF16)
        yield from unit_gather(bwd_all.at[c])

        for at in tiles(hidden):
            product = lax.dot_general(bwd_all[c], w_out[at, :], NT, preferred_element_type=F32)
            held = active[c, :, at].astype(F32)
            near[c, :, at] = jnp.where(held > 0.0, product, 0.0).astype(BF16)
        for at in tiles(D):
            product = lax.dot_general(near[c], w_in[at, :], NT, preferred_element_type=F32)
            bwd_own[c, :, at] = product[0 : 4 * part]
            bwd_part[c, :, at] = product.astype(BF16)
        grad_normed = yield from unit_sum(
            bwd_part.at[c], bwd_own.at[c], bwd_x.at[c], bwd_mid.at[c], bwd_z.at[c],
            bwd_turn.at[c], bwd_turn_mid.at[c], bwd_turn_in.at[c]
        )
        out_ref[here, :] = grad_sum_ref[c] + norm_back(
            grad_normed, inputs[here], scale_in[here], gain_in_ref[...]
        )

    chains = [chain(c) for c in chunks]
    for c in ORDER:
        next(chains[c], None)
    assert len(started) == SENDS
    for copy in started:
        copy.wait_send()


def local(x_rows, gain_in, w_in, w_out, gain_out, embed, targets, row_mask):
    block = x_rows.shape[2]
    part = block // CHUNKS
    rows = 16 * part
    hidden = w_in.shape[1]
    padded_vocab = (embed.shape[0] + 511) // 512 * 512
    c = CHUNKS
    unit_sum = [
        pltpu.VMEM((c, rows, D), BF16),
        pltpu.VMEM((c, rows, D), BF16),
        pltpu.VMEM((c, 4 * part, D), F32),
        pltpu.VMEM((c, 3, 4 * part, D), BF16),
        pltpu.VMEM((c, 4 * part, D), BF16),
        pltpu.VMEM((c, 3, part, D), BF16),
        pltpu.VMEM((c, 3, part, D - SPLIT), BF16),
        pltpu.VMEM((c, part, D - SPLIT), BF16),
        pltpu.VMEM((c, part, D - SPLIT), BF16),
    ]
    scratch = [
        pltpu.VMEM((block, D), BF16),
        pltpu.VMEM((1, D), F32),
        pltpu.VMEM((1, D), F32),
        pltpu.VMEM(targets.shape, jnp.int32),
        pltpu.VMEM(row_mask.shape, jnp.int32),
        pltpu.VMEM(w_in.shape, BF16),
        pltpu.VMEM(w_out.shape, BF16),
        pltpu.VMEM((padded_vocab, D), BF16),
        pltpu.VMEM((c, rows, hidden), BF16),
        pltpu.VMEM((c, rows, hidden), BF16),
        pltpu.VMEM((c, rows, padded_vocab), F32),
        pltpu.VMEM((c, rows, padded_vocab), BF16),
        pltpu.VMEM((c, rows, 1), F32),
        pltpu.VMEM((c, rows, 1), F32),
        *unit_sum,
        pltpu.VMEM((c, rows, D), BF16),
        pltpu.VMEM((c, 8, 128), F32),
        pltpu.VMEM((c, 15, 8, 128), F32),
        pltpu.VMEM((c, rows, D), BF16),
        pltpu.VMEM((c, rows // 2, D), BF16),
        pltpu.VMEM((c, rows // 2, D), BF16),
        pltpu.VMEM((c, 7, part, D), BF16),
        *unit_sum,
        pltpu.VMEM((c, part, D), F32),
        pltpu.VMEM((c, part, D), F32),
        pltpu.SemaphoreType.DMA((8,)),
        pltpu.SemaphoreType.DMA((SENDS,)),
        pltpu.SemaphoreType.DMA((SENDS,)),
    ]
    vmem = pl.BlockSpec(memory_space=pltpu.VMEM)
    anywhere = pl.BlockSpec(memory_space=pl.ANY)
    result = pl.pallas_call(
        kernel,
        out_shape=jax.ShapeDtypeStruct((block, D), F32),
        in_specs=[anywhere] * 8,
        out_specs=vmem,
        scratch_shapes=scratch,
        compiler_params=pltpu.CompilerParams(
            collective_id=0, has_side_effects=True, vmem_limit_bytes=56 * 1024 * 1024
        ),
        cost_estimate=pl.CostEstimate(
            flops=12 * 512 * D * hidden, bytes_accessed=6 * hidden * D, transcendentals=0
        ),
    )(
        x_rows.reshape(block, D), gain_in.reshape(1, D), w_in, w_out, gain_out.reshape(1, D), embed,
        targets, row_mask,
    )
    return result.reshape(1, 1, block, D)


def solution(mesh):
    in_specs = (
        P("vocab", "units", None, None),
        P(),
        P(None, "units"),
        P("units", None),
        P(),
        P("vocab", None),
        P(None, "units", None),
        P(None, "units", None),
    )
    out_specs = P("vocab", "units", None, None)
    return jax.shard_map(local, mesh=mesh, in_specs=in_specs, out_specs=out_specs, check_vma=False)
```
